32 devices in a mesh: seq: 8 (over z, y), head: 4 (over x, core).
Axes of the slice: x: 2, y: 2, z: 4, core: 2. Of those that a mesh axis runs over, the one named last changes fastest.
Arguments:
- queries: bfloat16 [1, 8192, 4096], P(None, ('seq', 'head')), may hold values from -4 to 4
- keys: bfloat16 [1, 8192, 4096], P(None, ('seq', 'head')), may hold values from -4 to 4
- values: bfloat16 [1, 8192, 4096], P(None, ('seq', 'head')), may hold values from -6 to 6
- features: bfloat16 [32, 256, 128], P('head'), may hold values from -4 to 4
Outputs:
- attended: bfloat16 [1, 8192, 4096], P(None, ('seq', 'head'))
The draws below stay inside these ranges and needn't reach their ends.
All inputs are finite; a program needn't handle non-finite values.
Results may differ from the reference program's by a relative error of at most 0.0065.
Values may be sent and summed in bfloat16 or wider, within the bound.
No kernel may reach another device: no remote copies, remote signals or barrier semaphores. Data moves between devices by JAX's collectives and lax.ppermute only.
A program may use at most 128 MiB of HBM per device.

```python
import math
import jax
import jax.numpy as jnp
from jax import lax

H = 32
DH = 128
M = 256
SEG = 1024
BATCH = 1
WIDTH = 4096
LENGTH = 8192


def shard_levels(key, dims, cuts, low, top_value):
    level, own = 1.0, jax.random.fold_in(key, 6)
    for axis_at, blocks in cuts:
        steps = jnp.exp(jax.random.uniform(jax.random.fold_in(own, axis_at), (blocks,), jnp.float32, low / len(cuts), top_value / len(cuts)))
        level = level * jnp.repeat(steps, dims[axis_at] // blocks).reshape([-1 if axis == axis_at else 1 for axis in range(len(dims))])
    return level


def gaussian(key, dims, width, reach, pieces=(), held_as=jnp.bfloat16):
    factor_of = shard_levels(key, dims, pieces, -0.22, 0.18) if pieces else 1.0
    values = jax.random.normal(key, dims, jnp.float32) * width * factor_of
    return jnp.minimum(jnp.maximum(values, -reach), reach).astype(held_as)


def setup_inputs(seed: int = 0) -> dict:
    streams_of = jax.random.split(jax.random.key(seed), 5)
    return {
        "queries": gaussian(streams_of[0], (BATCH, LENGTH, WIDTH), 1.0, 4.0, ((1, 32),)),
        "keys": gaussian(streams_of[1], (BATCH, LENGTH, WIDTH), 1.0, 4.0, ((1, 32),)),
        "values": gaussian(streams_of[2], (BATCH, LENGTH, WIDTH), 1.0, 6.0, ((1, 32),)),
        "features": gaussian(streams_of[3], (H, M, DH), 1.0, 4.0, ((0, 4),)),
    }


def feature_map(source, projection_directions):
    root_scale = DH ** (-0.25)
    widened = source.astype(jnp.float32)
    square_sum = lax.optimization_barrier(jnp.sum(widened * widened, axis=-1, keepdims=True))
    row_factor = lax.rsqrt(square_sum / DH + 1e-06)
    wide_dirs = projection_directions.astype(jnp.float32)
    dir_factor = lax.rsqrt(lax.optimization_barrier(jnp.mean(wide_dirs * wide_dirs, axis=-1)) + 1e-06)
    projected = jnp.dot(source, projection_directions.T, preferred_element_type=jnp.float32)
    projected = projected * row_factor * dir_factor[None, :] * root_scale
    halved = 0.5 * root_scale * root_scale * square_sum * row_factor * row_factor
    return (jnp.exp(projected - halved) * (1.0 / math.sqrt(M))).astype(jnp.bfloat16)

def reference(queries, keys, values, features):
    blocks = LENGTH // SEG
    causal_mask = jnp.tril(jnp.ones((SEG, SEG), dtype=bool))

    def one_pair(index):
        batch_index = index // H
        head_index = index % H
        start = (head_index * DH).astype(jnp.int32)
        head_query_rows = lax.dynamic_slice_in_dim(queries[batch_index], start, DH, 1)
        key_head = lax.dynamic_slice_in_dim(keys[batch_index], start, DH, 1)
        value_head = lax.dynamic_slice_in_dim(values[batch_index], start, DH, 1)
        projection_directions = features[head_index]
        phi_q = feature_map(head_query_rows, projection_directions).reshape(blocks, SEG, M)
        phi_k = feature_map(key_head, projection_directions).reshape(blocks, SEG, M)
        value_blocks = value_head.reshape(blocks, SEG, DH)

        def advance(carried, block_contents):
            states, totals = carried
            block_q, block_k, block_v = block_contents
            scores = jnp.dot(block_q, block_k.T, preferred_element_type=jnp.float32)
            scores = jnp.where(causal_mask, scores, jnp.float32(0.0))
            widened_query = block_q.astype(jnp.float32)
            denominator = lax.optimization_barrier(jnp.sum(scores, axis=1)) + jnp.dot(widened_query, totals, precision=lax.Precision.HIGHEST)
            weights = scores.astype(jnp.bfloat16)
            numerator_sum = jnp.dot(weights, block_v, preferred_element_type=jnp.float32)
            numerator_sum = numerator_sum + jnp.dot(widened_query, states, precision=lax.Precision.HIGHEST)
            result = (numerator_sum / denominator[:, None]).astype(jnp.bfloat16)
            states = states + jnp.dot(block_k.T, block_v, preferred_element_type=jnp.float32)
            totals = totals + lax.optimization_barrier(jnp.sum(block_k.astype(jnp.float32), axis=0))
            return ((states, totals), result)
        start_state = (jnp.zeros((M, DH), jnp.float32), jnp.zeros((M,), jnp.float32))
        unused, result_list = lax.scan(advance, start_state, (phi_q, phi_k, value_blocks))
        return result_list.reshape(LENGTH, DH)
    outputs = lax.map(one_pair, jnp.arange(BATCH * H, dtype=jnp.int32))
    outputs = outputs.reshape(BATCH, H, LENGTH, DH)
    return jnp.transpose(outputs, (0, 2, 1, 3)).reshape(BATCH, LENGTH, H * DH)
```

```python
import functools
import math

import jax
import jax.numpy as jnp
from jax import lax
from jax.experimental import pallas as pl
from jax.experimental.pallas import tpu as pltpu
from jax.sharding import PartitionSpec as P

F32, BF16 = jnp.float32, jnp.bfloat16
LOG2E = math.log2(math.e)
TOTAL_ROWS = 16
VMEM = 48 * 1024 * 1024


def feature_map(x, w):
    size, count = x.shape[1], w.shape[0]
    c = size ** (-0.25)
    p = lax.dot_general(x, w, (((1,), (1,)), ((), ())), preferred_element_type=F32)
    wide = x.astype(F32)
    square = jnp.sum(wide * wide, axis=1, keepdims=True)
    r = lax.rsqrt(square / size + 1e-06)
    half = square * r * r * (0.5 * c * c * LOG2E) + 0.5 * math.log2(count)
    ww = w.astype(F32)
    ww = ww * ww
    high = ww.astype(BF16)
    low = (ww - high.astype(F32)).astype(BF16)
    ones = jnp.ones((16, size), BF16)
    nt = (((1,), (1,)), ((), ()))
    total = lax.dot_general(ones, high, nt, preferred_element_type=F32)
    total = total + lax.dot_general(ones, low, nt, preferred_element_type=F32)
    s = lax.rsqrt(total[:1] / size + 1e-06)
    return jnp.exp2(p * (r * (c * LOG2E)) * s - half).astype(BF16)


def pick(first, f0, f1, h):
    return jnp.where(first, f0[h], f1[h])


def states_kernel(group, size, pos, k, v, f0, f1, phi, state):
    first = pl.program_id(0) == 0
    rows = []
    for h in range(group):
        cols = slice(h * size, (h + 1) * size)
        ph = feature_map(k[:, cols], pick(first, f0, f1, h))
        phi[0, 0, h] = ph
        st = lax.dot_general(
            v[:, cols], ph, (((0,), (0,)), ((), ())), preferred_element_type=F32
        )
        state[0, 0, h * size : (h + 1) * size] = st.astype(BF16)
        rows.append(jnp.sum(ph.astype(F32), axis=0, keepdims=True))
    rows.append(jnp.zeros((TOTAL_ROWS - group, rows[0].shape[1]), F32))
    state[0, 0, group * size :] = jnp.concatenate(rows, axis=0).astype(BF16)


def weights_kernel(group, size, pos, q, f0, f1, phi_k, phi_q, weights):
    first = pl.program_id(0) == 0
    tokens = q.shape[0]
    row = lax.broadcasted_iota(jnp.int32, (tokens, tokens), 0)
    col = lax.broadcasted_iota(jnp.int32, (tokens, tokens), 1)
    mask = col <= row
    for h in range(group):
        cols = slice(h * size, (h + 1) * size)
        ph = feature_map(q[:, cols], pick(first, f0, f1, h))
        phi_q[0, 0, h] = ph
        sc = lax.dot_general(
            ph, phi_k[0, 0, h], (((1,), (1,)), ((), ())), preferred_element_type=F32
        )
        weights[0, 0, h] = jnp.where(mask, sc, 0.0).astype(BF16)


def output_kernel(group, size, parts, pos, phi_q, weights, v, other, *rest):
    pieces, out, held = rest[: 2 * parts], rest[-2], rest[-1]
    step = pl.program_id(0) * parts + pl.program_id(1)
    add = (pos[1] == 1).astype(F32)
    for i in range(2 * parts):

        @pl.when(step == i)
        def _():
            held[...] = pieces[i][...].astype(F32) + add * other[0, 0].astype(F32)

    tokens, count = phi_q.shape[-2:]
    ones = jnp.ones((tokens, size), BF16)
    for h in range(group):
        cols = slice(h * size, (h + 1) * size)
        st = held[h * size : (h + 1) * size].astype(BF16)
        tot = held[group * size + h : group * size + h + 1]
        tot = jnp.broadcast_to(tot, (size, count)).astype(BF16)
        acc = lax.dot_general(
            phi_q[0, 0, h],
            jnp.concatenate([st, tot], axis=0),
            (((1,), (1,)), ((), ())),
            preferred_element_type=F32,
        )
        acc = acc + jnp.dot(
            weights[0, 0, h],
            jnp.concatenate([v[:, cols], ones], axis=1),
            preferred_element_type=F32,
        )
        out[:, cols] = (acc[:, :size] / acc[:, size:]).astype(BF16)


def body(seqs, heads, queries, keys, values, features):
    tokens, width = queries.shape[1:]
    q, k, v = (a.reshape(tokens, width) for a in (queries, keys, values))
    own, count, size = features.shape
    cores = 2
    nx = heads // cores
    ny = nx if seqs % nx == 0 else 1
    nz = seqs // ny
    flip = 1 if nx > 1 else 0
    group = own // ny
    srows = group * size
    rows = srows + TOTAL_ROWS

    hi, si = lax.axis_index("head"), lax.axis_index("seq")
    x, c = hi // cores, hi % cores
    z, y = si // ny, si % ny
    pos = jnp.stack([x, c, y]).astype(jnp.int32)

    def head_swap(a, bits):
        return lax.ppermute(a, "head", [(i, i ^ bits) for i in range(heads)])

    def seq_swap(a, bits):
        return lax.ppermute(a, "seq", [(i, i ^ bits) for i in range(seqs)])

    def plane_swap(a, dx, dy):
        if dy == 0:
            return head_swap(a, dx * cores)
        if dx == 0:
            return seq_swap(a, dy)
        pairs = [
            (s * heads + h, (s ^ dy) * heads + (h ^ (dx * cores)))
            for s in range(seqs)
            for h in range(heads)
        ]
        return lax.ppermute(a, ("seq", "head"), pairs)

    def column(dx):
        return lambda i, j, p: (
            0,
            ((p[0] ^ dx ^ flip) * cores + (p[1] ^ i)) * ny + (p[2] ^ j),
        )

    def feature_specs():
        shape = (group, count, size)
        return [
            pl.BlockSpec(shape, lambda i, j, p: (jnp.where(i == 0, p[2] ^ j, p[2] ^ (ny - 1)), 0, 0)),
            pl.BlockSpec(shape, lambda i, j, p: (jnp.where(i == 1, p[2] ^ j, p[2]), 0, 0)),
        ]

    def per_head(a, b):
        return pl.BlockSpec((1, 1, group, a, b), lambda i, j, p: (i, j, 0, 0, 0))

    def call(kernel, ins, outs, shapes, flops, extra=(), alias={}):
        return pl.pallas_call(
            kernel,
            out_shape=shapes,
            grid_spec=pltpu.PrefetchScalarGridSpec(
                num_scalar_prefetch=1,
                grid=(cores, ny),
                in_specs=ins,
                out_specs=outs,
                scratch_shapes=extra,
            ),
            input_output_aliases=alias,
            compiler_params=pltpu.CompilerParams(vmem_limit_bytes=VMEM),
            cost_estimate=pl.CostEstimate(
                flops=flops, bytes_accessed=8 << 20, transcendentals=0
            ),
        )

    def token_spec(dx):
        return pl.BlockSpec((tokens, group * size), column(dx))

    dirs = {}
    for ox in range(nx):
        mine = features if ox == 0 else head_swap(features, ox * cores)
        dirs[ox] = (mine, head_swap(mine, 1))

    def states(dx):
        f0, f1 = dirs[dx ^ flip]
        return call(
            functools.partial(states_kernel, group, size),
            [token_spec(dx), token_spec(dx), *feature_specs()],
            [per_head(tokens, count), pl.BlockSpec((1, 1, rows, count), lambda i, j, p: (i, j, 0, 0))],
            [
                jax.ShapeDtypeStruct((cores, ny, group, tokens, count), BF16),
                jax.ShapeDtypeStruct((cores, ny, rows, count), BF16),
            ],
            2 * 2 * tokens * count * size * own * cores,
        )(pos, k, v, f0, f1)

    def weights(dx, phi_k):
        f0, f1 = dirs[dx ^ flip]
        return call(
            functools.partial(weights_kernel, group, size),
            [token_spec(dx), *feature_specs(), per_head(tokens, count)],
            [per_head(tokens, count), per_head(tokens, tokens)],
            [
                jax.ShapeDtypeStruct((cores, ny, group, tokens, count), BF16),
                jax.ShapeDtypeStruct((cores, ny, group, tokens, tokens), BF16),
            ],
            2 * tokens * count * (size + tokens) * own * cores,
        )(pos, q, f0, f1, phi_k)

    order_x = [flip] + [dx for dx in range(nx) if dx != flip]
    phi_k, other, piece, got = {}, {}, {}, {}
    for dx in order_x:
        phi_k[dx], state = states(dx)
        other[dx] = head_swap(state, 1)
        for dy in range(ny):
            t = state[0, dy].astype(F32) + other[dx][1, dy].astype(F32)
            piece[dx, dy] = t.astype(BF16)
        for dy in range(ny):
            if (dx, dy) != (0, 0):
                got[dx, dy] = plane_swap(piece[dx, dy], dx, dy)
    got[0, 0] = piece[0, 0]

    wide = {key: a.astype(F32) for key, a in got.items()}
    plane = functools.reduce(lambda a, b: a + b, wide.values()).astype(BF16)
    zrows = srows // nz
    plane_totals = plane[srows:]
    heard = []
    for j in range(nz):
        part = lax.dynamic_slice_in_dim(plane, (z ^ j) * zrows, zrows, 0)
        part = jnp.concatenate([part, plane_totals], axis=0)
        heard.append(part if j == 0 else seq_swap(part, j * ny))
    heard_wide = [a.astype(F32) for a in heard]

    def before(target):
        total = 0.0
        for j in range(nz):
            total = total + jnp.where((z ^ j) < target, heard_wide[j], 0.0)
        return total

    prefix = []
    for j in range(nz):
        e = before(z ^ j)[:zrows].astype(BF16)
        prefix.append(e if j == 0 else seq_swap(e, j * ny))
    parts = []
    for p in range(nz):
        part = prefix[0]
        for j in range(1, nz):
            part = jnp.where((z ^ j) == p, prefix[j], part)
        parts.append(part.astype(F32))
    base = jnp.concatenate([*parts, before(z)[zrows:]], axis=0)

    place = y * nx + x
    result = {}
    for dx, dy in got:
        target = (y ^ dy) * nx + (x ^ dx)
        total = base
        for ex, ey in got:
            source = (y ^ ey) * nx + (x ^ ex)
            total = total + jnp.where(source < target, wide[ex, ey], 0.0)
        total = total.astype(BF16)
        result[dx, dy] = total if (dx, dy) == (0, 0) else plane_swap(total, dx, dy)

    phi_w = {dx: weights(dx, phi_k[dx]) for dx in order_x}

    out = None
    for dx in range(nx):
        near = [result[dx, dy] for dy in range(ny)]
        far = [head_swap(a, 1) for a in near]
        whole = pl.BlockSpec((rows, count), lambda i, j, p: (0, 0))
        args = [pos, *phi_w[dx], v, other[dx], *near, *far]
        specs = [
            per_head(tokens, count),
            per_head(tokens, tokens),
            token_spec(dx),
            pl.BlockSpec((1, 1, rows, count), lambda i, j, p: (1 - i, j, 0, 0)),
            *[whole] * (cores * ny),
        ]
        kernel = functools.partial(output_kernel, group, size, ny)
        alias = {}
        if out is not None:
            args.append(out)
            specs.append(pl.BlockSpec(memory_space=pl.ANY))
            alias = {len(args) - 1: 0}
        out = call(
            kernel,
            specs,
            token_spec(dx),
            jax.ShapeDtypeStruct((tokens, width), BF16),
            2 * 2 * tokens * count * (2 * size) * own * cores,
            [pltpu.VMEM((rows, count), F32)],
            alias,
        )(*args)
    return out.reshape(queries.shape)


def solution(mesh):
    token = P(None, ("seq", "head"), None)
    return jax.shard_map(
        functools.partial(body, mesh.shape["seq"], mesh.shape["head"]),
        mesh=mesh,
        in_specs=(token, token, token, P("head", None, None)),
        out_specs=token,
        check_vma=False,
    )
```

```python
import functools
import math

import jax
import jax.numpy as jnp
from jax import lax
from jax.experimental import pallas as pl
from jax.experimental.pallas import tpu as pltpu
from jax.sharding import PartitionSpec as P

F32, BF16 = jnp.float32, jnp.bfloat16
LOG2E = math.log2(math.e)
TOTAL_ROWS = 16
VMEM = 12 * 1024 * 1024


def feature_map(x, w):
    size, count = x.shape[1], w.shape[0]
    c = size ** (-0.25)
    p = lax.dot_general(x, w, (((1,), (1,)), ((), ())), preferred_element_type=F32)
    wide = x.astype(F32)
    square = jnp.sum(wide * wide, axis=1, keepdims=True)
    r = lax.rsqrt(square / size + 1e-06)
    half = square * r * r * (0.5 * c * c * LOG2E) + 0.5 * math.log2(count)
    ww = w.astype(F32)
    ww = ww * ww
    high = ww.astype(BF16)
    low = (ww - high.astype(F32)).astype(BF16)
    ones = jnp.ones((16, size), BF16)
    nt = (((1,), (1,)), ((), ()))
    total = lax.dot_general(ones, high, nt, preferred_element_type=F32)
    total = total + lax.dot_general(ones, low, nt, preferred_element_type=F32)
    s = lax.rsqrt(total[:1] / size + 1e-06)
    return jnp.exp2(p * (r * (c * LOG2E)) * s - half).astype(BF16)


def place_of(pos, key, nx, ny, core):
    flip = 1 if nx > 1 else 0
    part = pos[2] ^ key[1]
    return ((pos[0] ^ key[0] ^ flip) * 2 + (pos[1] ^ core)) * ny + part, part


def heads_of(pos, key, shape, f0, f1):
    nx, ny, group, size = shape
    for core, f in ((1, f1), (0, f0)):
        place, part = place_of(pos, key, nx, ny, core)
        first = 0 if f.shape[0] == group else part * group
        for h in range(group):
            start = pl.multiple_of((place * group + h) * size, size)
            yield (1 - core) * group + h, pl.ds(start, size), f, first + h


def states_kernel(key, shape, pos, k, v, f0, f1, *rest):
    phi, other, mine = rest[-3:]
    group, size = shape[2:]
    heads = list(heads_of(pos, key, shape, f0, f1))
    totals = []
    for i, cols, f, at in heads:
        ph = feature_map(k[:, cols], f[at])
        phi[i] = ph
        totals.append(jnp.sum(ph.astype(F32), axis=0, keepdims=True))
    for i, cols, _, _ in heads:
        out, h = (mine if i >= group else other), i % group
        st = lax.dot_general(
            v[:, cols], phi[i], (((0,), (0,)), ((), ())), preferred_element_type=F32
        )
        out[h * size : (h + 1) * size] = st.astype(BF16)
    pad = jnp.zeros((TOTAL_ROWS - group, totals[0].shape[1]), F32)
    other[group * size :] = jnp.concatenate([*totals[:group], pad], axis=0).astype(BF16)
    mine[group * size :] = jnp.concatenate([*totals[group:], pad], axis=0).astype(BF16)


def weights_kernel(key, shape, pos, q, f0, f1, phi_k, *rest):
    phi_q, weights = rest[-2:]
    tokens = q.shape[0]
    heads = list(heads_of(pos, key, shape, f0, f1))
    for i, cols, f, at in heads:
        phi_q[i] = feature_map(q[:, cols], f[at])
    row = lax.broadcasted_iota(jnp.int32, (tokens, tokens), 0)
    col = lax.broadcasted_iota(jnp.int32, (tokens, tokens), 1)
    mask = col <= row
    for i, _, _, _ in heads:
        sc = lax.dot_general(
            phi_q[i], phi_k[i], (((1,), (1,)), ((), ())), preferred_element_type=F32
        )
        weights[i] = jnp.where(mask, sc, 0.0).astype(BF16)


def output_kernel(key, shape, pos, phi_q, weights, v, far, far_add, near, near_add, *rest):
    out, held, ready, sems = rest[-4:]
    nx, ny, group, size = shape
    tokens, count = phi_q.shape[-2:]
    add = (pos[1] == 1).astype(F32)
    ones = jnp.ones((tokens, size), BF16)
    copies = []
    for half, (base, extra) in enumerate(((far, far_add), (near, near_add))):
        place = place_of(pos, key, nx, ny, 1 - half)[0]
        held[half] = (base[...].astype(F32) + add * extra[...].astype(F32)).astype(BF16)
        totals = held[half, group * size :].astype(F32)
        for h in range(group):
            st = held[half, h * size : (h + 1) * size]
            tot = jnp.broadcast_to(totals[h : h + 1], (size, count)).astype(BF16)
            acc = lax.dot_general(
                phi_q[half * group + h],
                jnp.concatenate([st, tot], axis=0),
                (((1,), (1,)), ((), ())),
                preferred_element_type=F32,
            )
            start = pl.multiple_of((place * group + h) * size, size)
            acc = acc + jnp.dot(
                weights[half * group + h],
                jnp.concatenate([v[:, pl.ds(start, size)], ones], axis=1),
                preferred_element_type=F32,
            )
            ready[half, :, h * size : (h + 1) * size] = (acc[:, :size] / acc[:, size:]).astype(BF16)
        wide = group * size
        copy = pltpu.make_async_copy(
            ready.at[half],
            out.at[:, pl.ds(pl.multiple_of(place * wide, wide), wide)],
            sems.at[half],
        )
        copy.start()
        copies.append(copy)
    for copy in copies:
        copy.wait()


def plane_kernel(count, zrows, pos, *refs):
    held, z = refs[-1], pos[3]
    pieces, outs = refs[:count], refs[-1 - (held.shape[0] - TOTAL_ROWS) // zrows : -1]
    total = pieces[0][...].astype(F32)
    for piece in pieces[1:]:
        total = total + piece[...].astype(F32)
    held[...] = total
    srows = len(outs) * zrows
    for j, out in enumerate(outs):
        start = pl.multiple_of((z ^ j) * zrows, zrows)
        out[:zrows] = held[pl.ds(start, zrows)].astype(BF16)
        out[zrows:] = held[srows:].astype(BF16)


def prefix_kernel(count, zrows, pos, *refs):
    heard, outs, totals = refs[:count], refs[-1 - count : -1], refs[-1]
    z = pos[3]
    for j, out in enumerate(outs):
        total = jnp.zeros(out.shape, F32)
        for i, part in enumerate(heard):
            total = total + jnp.where((z ^ i) < (z ^ j), part[:zrows].astype(F32), 0.0)
        out[...] = total.astype(BF16)
    total = jnp.zeros(totals.shape, F32)
    for i, part in enumerate(heard):
        total = total + jnp.where((z ^ i) < z, part[zrows:].astype(F32), 0.0)
    totals[...] = total


def place_kernel(nx, ny, count, zrows, pos, *refs):
    keys = [(dx, dy) for dx in range(nx) for dy in range(ny)]
    prefix, totals = refs[:count], refs[count]
    pieces, outs = refs[count + 1 : count + 1 + len(keys)], refs[-1 - len(keys) : -1]
    held = refs[-1]
    x, y, z = pos[0], pos[2], pos[3]
    for j in range(count):
        start = pl.multiple_of((z ^ j) * zrows, zrows)
        held[pl.ds(start, zrows)] = prefix[j][...].astype(F32)
    held[count * zrows :] = totals[...]
    for (dx, dy), out in zip(keys, outs):
        target = (y ^ dy) * nx + (x ^ dx)
        total = held[...]
        for (ex, ey), piece in zip(keys, pieces):
            source = (y ^ ey) * nx + (x ^ ex)
            total = total + jnp.where(source < target, piece[...].astype(F32), 0.0)
        out[...] = total.astype(BF16)


def body(seqs, heads, queries, keys, values, features):
    tokens, width = queries.shape[1:]
    q, k, v = (a.reshape(tokens, width) for a in (queries, keys, values))
    own, count, size = features.shape
    cores = 2
    nx = heads // cores
    ny = nx if seqs % nx == 0 else 1
    nz = seqs // ny
    flip = 1 if nx > 1 else 0
    group = own // ny
    srows = group * size
    zrows = srows // nz
    rows = srows + TOTAL_ROWS
    plane = [(dx, dy) for dx in range(nx) for dy in range(ny)]

    hi, si = lax.axis_index("head"), lax.axis_index("seq")
    x, c = hi // cores, hi % cores
    z, y = si // ny, si % ny
    pos = jnp.stack([x, c, y, z]).astype(jnp.int32)

    def head_swap(a, bits):
        return lax.ppermute(a, "head", [(i, i ^ bits) for i in range(heads)])

    def seq_swap(a, bits):
        return lax.ppermute(a, "seq", [(i, i ^ bits) for i in range(seqs)])

    def plane_swap(a, dx, dy):
        if dy == 0:
            return head_swap(a, dx * cores)
        if dx == 0:
            return seq_swap(a, dy)
        pairs = [
            (s * heads + h, (s ^ dy) * heads + (h ^ (dx * cores)))
            for s in range(seqs)
            for h in range(heads)
        ]
        return lax.ppermute(a, ("seq", "head"), pairs)

    anywhere = pl.BlockSpec(memory_space=pl.ANY)

    shape = (nx, ny, group, size)
    near, smem = pl.BlockSpec(memory_space=pltpu.VMEM), pl.BlockSpec(memory_space=pltpu.SMEM)

    def call(kernel, out, args, after=(), outs=near, scratch=(), alias={}):
        return pl.pallas_call(
            kernel,
            out_shape=out,
            in_specs=[smem] + [near] * len(args) + [anywhere] * len(after),
            out_specs=jax.tree.map(lambda _: outs, out),
            scratch_shapes=scratch,
            input_output_aliases=alias,
            compiler_params=pltpu.CompilerParams(vmem_limit_bytes=VMEM),
        )(pos, *args, *after)

    def per_head(a, b):
        return jax.ShapeDtypeStruct((cores * group, a, b), BF16)

    whole = jax.ShapeDtypeStruct((rows, count), BF16)

    dirs, phi_k, phi_w, piece, got, theirs = {}, {}, {}, {}, {}, {}

    def states(key, after=()):
        phi_k[key], other, mine = call(
            functools.partial(states_kernel, key, shape),
            [per_head(tokens, count), whole, whole],
            [k, v, *dirs[key]],
            after,
        )
        theirs[key] = [head_swap(other, 1), head_swap(mine, 1)]
        piece[key] = (mine.astype(F32) + theirs[key][0].astype(F32)).astype(BF16)
        got[key] = piece[key] if key == (0, 0) else plane_swap(piece[key], *key)
        return mine

    def weights(key, after=()):
        phi_w[key] = call(
            functools.partial(weights_kernel, key, shape),
            [per_head(tokens, count), per_head(tokens, tokens)],
            [q, *dirs[key], phi_k[key]],
            after,
        )
        return phi_w[key][0]

    near_dirs = head_swap(features, 1)
    for dy in range(ny):
        dirs[flip, dy] = (features, near_dirs)
    for ox in range(1, nx):
        if ny == 2:
            part = lax.dynamic_slice_in_dim(features, (y ^ 1) * group, group, 0)
            part = head_swap(part, ox * cores)
            rest = seq_swap(part, 1)
            dirs[ox ^ flip, 1] = (part, head_swap(part, 1))
            dirs[ox ^ flip, 0] = (rest, head_swap(rest, 1))
        else:
            full = head_swap(features, ox * cores)
            full = (full, head_swap(full, 1))
            for dy in range(ny):
                dirs[ox ^ flip, dy] = full

    first = [(flip, dy) for dy in range(ny)]
    later = [(dx, dy) for dx in range(nx) for dy in reversed(range(ny)) if dx != flip]
    for key in first:
        last = states(key)
    for i, key in enumerate(later):
        last = states(key, [piece[first[min(i, ny - 1)]]])

    done = weights(first[0], [last])
    summed = call(
        functools.partial(plane_kernel, len(plane), zrows),
        [jax.ShapeDtypeStruct((zrows + TOTAL_ROWS, count), BF16)] * nz,
        [got[key] for key in plane],
        [done],
        scratch=[pltpu.VMEM((rows, count), F32)],
    )
    heard = [a if j == 0 else seq_swap(a, j * ny) for j, a in enumerate(summed)]
    done = [weights(key, [summed[-1]]) for key in [*first[1:], *later[:-1]]]
    *prefix, totals = call(
        functools.partial(prefix_kernel, nz, zrows),
        [jax.ShapeDtypeStruct((zrows, count), BF16)] * nz
        + [jax.ShapeDtypeStruct((TOTAL_ROWS, count), F32)],
        heard,
        done,
    )
    done = [weights(later[-1], [prefix[-1]])] if later else []
    prefix = [a if j == 0 else seq_swap(a, j * ny) for j, a in enumerate(prefix)]
    placed = call(
        functools.partial(place_kernel, nx, ny, nz, zrows),
        [whole] * len(plane),
        [*prefix, totals, *[got[key] for key in plane]],
        done,
        scratch=[pltpu.VMEM((rows, count), F32)],
    )

    out = None
    for key, base in zip(plane, placed):
        if key != (0, 0):
            base = plane_swap(base, *key)
        args = [*phi_w[key], v, head_swap(base, 1), theirs[key][1], base, theirs[key][0]]
        out = call(
            functools.partial(output_kernel, key, shape),
            jax.ShapeDtypeStruct((tokens, width), BF16),
            args,
            [] if out is None else [out],
            anywhere,
            [
                pltpu.VMEM((cores, rows, count), BF16),
                pltpu.VMEM((cores, tokens, group * size), BF16),
                pltpu.SemaphoreType.DMA((cores,)),
            ],
            {} if out is None else {1 + len(args): 0},
        )
    return out.reshape(queries.shape)


def solution(mesh):
    token = P(None, ("seq", "head"), None)
    return jax.shard_map(
        functools.partial(body, mesh.shape["seq"], mesh.shape["head"]),
        mesh=mesh,
        in_specs=(token, token, token, P("head", None, None)),
        out_specs=token,
        check_vma=False,
    )
```

```python
import functools
import math

import jax
import jax.numpy as jnp
from jax import lax
from jax.experimental import pallas as pl
from jax.experimental.pallas import tpu as pltpu
from jax.sharding import PartitionSpec as P

F32, BF16 = jnp.float32, jnp.bfloat16
LOG2E = math.log2(math.e)
TOTAL_ROWS = 16
VMEM = 12 * 1024 * 1024


def feature_map(x, w):
    size, count = x.shape[1], w.shape[0]
    c = size ** (-0.25)
    p = lax.dot_general(x, w, (((1,), (1,)), ((), ())), preferred_element_type=F32)
    wide = x.astype(F32)
    square = jnp.sum(wide * wide, axis=1, keepdims=True)
    r = lax.rsqrt(square / size + 1e-06)
    half = square * r * r * (0.5 * c * c * LOG2E) + 0.5 * math.log2(count)
    ww = w.astype(F32)
    ww = ww * ww
    high = ww.astype(BF16)
    low = (ww - high.astype(F32)).astype(BF16)
    ones = jnp.ones((16, size), BF16)
    nt = (((1,), (1,)), ((), ()))
    total = lax.dot_general(ones, high, nt, preferred_element_type=F32)
    total = total + lax.dot_general(ones, low, nt, preferred_element_type=F32)
    s = lax.rsqrt(total[:1] / size + 1e-06)
    return jnp.exp2(p * (r * (c * LOG2E)) * s - half).astype(BF16)


def position(nx, ny):
    head, seq = lax.axis_index("head"), lax.axis_index("seq")
    return head // 2, head % 2, seq % ny, seq // ny


def place_of(pos, key, nx, ny, core):
    flip = 1 if nx > 1 else 0
    part = pos[2] ^ key[1]
    return ((pos[0] ^ key[0] ^ flip) * 2 + (pos[1] ^ core)) * ny + part, part


def heads_of(pos, key, shape, f0, f1):
    nx, ny, group, size = shape
    for core, f in ((1, f1), (0, f0)):
        place, part = place_of(pos, key, nx, ny, core)
        first = 0 if f.shape[0] == group else part * group
        for h in range(group):
            start = pl.multiple_of((place * group + h) * size, size)
            yield (1 - core) * group + h, pl.ds(start, size), f, first + h


def states_kernel(key, shape, waits, k, v, f0, f1, phi, *sums):
    nx, ny, group, size = shape
    *others, mine = sums
    pos = position(nx, ny)
    heads = list(heads_of(pos, key, shape, f0, f1))
    totals = []
    for i, cols, f, at in heads:
        if i % group == 0:
            waits(i // group)
        ph = feature_map(k[:, cols], f[at])
        phi[i] = ph
        totals.append(jnp.sum(ph.astype(F32), axis=0, keepdims=True))
    waits(2)
    for i, cols, _, _ in heads:
        h, half = i % group, group // 2
        late = i < group and h >= half
        out = mine if i >= group else others[-1] if late else others[0]
        h = h - half if late else h
        st = lax.dot_general(
            v[:, cols], phi[i], (((0,), (0,)), ((), ())), preferred_element_type=F32
        )
        out[h * size : (h + 1) * size] = st.astype(BF16)
    pad = jnp.zeros((TOTAL_ROWS - group, totals[0].shape[1]), F32)
    others[-1][(group - group // 2) * size :] = jnp.concatenate([*totals[:group], pad], axis=0).astype(BF16)
    mine[group * size :] = jnp.concatenate([*totals[group:], pad], axis=0).astype(BF16)
    waits(3)


def first_kernel(key, shape, k_far, v_far, f_far, f1, *refs):
    nx, ny, group, size = shape
    *outs, k, v, f, sems = refs
    wide = group * size
    blocks = k.shape[1] // wide
    place = place_of(position(nx, ny), key, nx, ny, 0)[0]
    copies = [[], [], [], []]

    def fetch(stage, source, target, at):
        copy = pltpu.make_async_copy(source, target, sems.at[at])
        copy.start()
        copies[stage].append(copy)

    def fetch_block(stage, source, target, j, at):
        cols = pl.ds(pl.multiple_of((place ^ j) * wide, wide), wide)
        fetch(stage, source.at[:, cols], target.at[:, cols], at)

    fetch_block(0, k_far, k, ny, 1)
    fetch(1, f_far, f, 0)
    fetch_block(1, k_far, k, 0, 2)
    fetch_block(2, v_far, v, ny, blocks + 1)
    fetch_block(2, v_far, v, 0, blocks + 2)
    rest = [j for j in range(blocks) if j not in (0, ny)]
    for n, j in enumerate(rest):
        fetch_block(3, k_far, k, j, 3 + n)
        fetch_block(3, v_far, v, j, blocks + 3 + n)

    def waits(stage):
        for copy in copies[stage]:
            copy.wait()

    states_kernel(key, shape, waits, k, v, f, f1, *outs)


def second_kernel(key, shape, q_far, k, v, f0, f1, *refs):
    *outs, q, sem = refs
    copy = pltpu.make_async_copy(q_far, q, sem.at[0])
    copy.start()

    def waits(stage):
        if stage == 3:
            copy.wait()

    states_kernel(key, shape, waits, k, v, f0, f1, *outs)


def later_kernel(extra, key, shape, k, v, f0, f1, *refs):
    states_kernel(key, shape, lambda stage: None, k, v, f0, f1, *refs[extra:])


def inner_kernel(key, shape, q, v, f0, f1, phi_k, *rest):
    phi_q, inner, weights = rest[-3:]
    nx, ny, group, size = shape
    tokens = q.shape[0]
    heads = list(heads_of(position(nx, ny), key, shape, f0, f1))
    for i, cols, f, at in heads:
        phi_q[i] = feature_map(q[:, cols], f[at])
    row = lax.broadcasted_iota(jnp.int32, (tokens, tokens), 0)
    col = lax.broadcasted_iota(jnp.int32, (tokens, tokens), 1)
    mask = col <= row
    for i, _, _, _ in heads:
        sc = lax.dot_general(
            phi_q[i], phi_k[i], (((1,), (1,)), ((), ())), preferred_element_type=F32
        )
        weights[i] = jnp.where(mask, sc, 0.0).astype(BF16)
    ones = jnp.ones((tokens, size), BF16)
    for i, cols, _, _ in heads:
        inner[i] = jnp.dot(
            weights[i],
            jnp.concatenate([v[:, cols], ones], axis=1),
            preferred_element_type=F32,
        )


def output_kernel(jobs, shape, *refs):
    out, ready, sems = refs[-3:]
    nx, ny, group, size = shape
    pos = position(nx, ny)
    add = (pos[1] == 1).astype(F32)
    copies = []
    for n, (key, core) in enumerate(jobs):
        phi_q, inner, base, extra_a, extra_b = refs[5 * n : 5 * n + 5]
        count = phi_q.shape[-1]
        place = place_of(pos, key, nx, ny, core)[0]
        half = extra_a.shape[0]
        whole = half == base.shape[0]
        last = extra_a[group * size :] if whole else extra_b[group * size - half :]
        totals = base[group * size :].astype(F32) + add * last.astype(F32)
        for h in range(group):
            rows = slice(h * size, (h + 1) * size)
            if whole or h * size < half:
                extra = extra_a[rows]
            else:
                extra = extra_b[h * size - half : (h + 1) * size - half]
            st = (base[rows].astype(F32) + add * extra.astype(F32)).astype(BF16)
            tot = jnp.broadcast_to(totals[h : h + 1], (size, count)).astype(BF16)
            at = (1 - core) * group + h
            acc = inner[at] + lax.dot_general(
                phi_q[at],
                jnp.concatenate([st, tot], axis=0),
                (((1,), (1,)), ((), ())),
                preferred_element_type=F32,
            )
            ready[n, :, rows] = (acc[:, :size] / acc[:, size:]).astype(BF16)
        wide = group * size
        copy = pltpu.make_async_copy(
            ready.at[n],
            out.at[:, pl.ds(pl.multiple_of(place * wide, wide), wide)],
            sems.at[n],
        )
        copy.start()
        copies.append(copy)
    for copy in copies:
        copy.wait()


def tie_kernel(count, *refs):
    for a, out in zip(refs[:count], refs[-count:]):
        out[...] = a[...]


def chip_kernel(mine, *refs):
    *others, out = refs
    start = 0
    for other in others:
        rows = slice(start, start + other.shape[0])
        start = rows.stop
        out[rows] = (mine[rows].astype(F32) + other[...].astype(F32)).astype(BF16)


def plane_kernel(count, zrows, ny, *refs):
    held, z = refs[-1], position(1, ny)[3]
    pieces, outs = refs[:count], refs[-1 - (held.shape[0] - TOTAL_ROWS) // zrows : -1]
    total = pieces[0][...].astype(F32)
    for piece in pieces[1:]:
        total = total + piece[...].astype(F32)
    held[...] = total
    srows = len(outs) * zrows
    for j, out in enumerate(outs):
        start = pl.multiple_of((z ^ j) * zrows, zrows)
        out[:zrows] = held[pl.ds(start, zrows)].astype(BF16)
        out[zrows:] = held[srows:].astype(BF16)


def prefix_kernel(count, zrows, ny, *refs):
    heard, outs, totals = refs[:count], refs[-1 - count : -1], refs[-1]
    z = position(1, ny)[3]
    for j, out in enumerate(outs):
        total = jnp.zeros(out.shape, F32)
        for i, part in enumerate(heard):
            total = total + jnp.where((z ^ i) < (z ^ j), part[:zrows].astype(F32), 0.0)
        out[...] = total.astype(BF16)
    total = jnp.zeros(totals.shape, F32)
    for i, part in enumerate(heard):
        total = total + jnp.where((z ^ i) < z, part[zrows:].astype(F32), 0.0)
    totals[...] = total


def place_kernel(nx, ny, count, zrows, *refs):
    keys = [(dx, dy) for dx in range(nx) for dy in range(ny)]
    prefix, totals = refs[:count], refs[count]
    pieces, outs = refs[count + 1 : count + 1 + len(keys)], refs[-1 - len(keys) : -1]
    held = refs[-1]
    x, _, y, z = position(nx, ny)
    for j in range(count):
        start = pl.multiple_of((z ^ j) * zrows, zrows)
        held[pl.ds(start, zrows)] = prefix[j][...].astype(F32)
    held[count * zrows :] = totals[...]
    for (dx, dy), out in zip(keys, outs):
        target = (y ^ dy) * nx + (x ^ dx)
        total = held[...]
        for (ex, ey), piece in zip(keys, pieces):
            source = (y ^ ey) * nx + (x ^ ex)
            total = total + jnp.where(source < target, piece[...].astype(F32), 0.0)
        out[...] = total.astype(BF16)


def body(seqs, heads, queries, keys, values, features):
    tokens, width = queries.shape[1:]
    q, k, v = (a.reshape(tokens, width) for a in (queries, keys, values))
    own, count, size = features.shape
    cores = 2
    nx = heads // cores
    ny = nx if seqs % nx == 0 else 1
    nz = seqs // ny
    flip = 1 if nx > 1 else 0
    group = own // ny
    srows = group * size
    zrows = srows // nz
    rows = srows + TOTAL_ROWS
    plane = [(dx, dy) for dx in range(nx) for dy in range(ny)]

    y = position(nx, ny)[2]

    def head_swap(a, bits):
        return lax.ppermute(a, "head", [(i, i ^ bits) for i in range(heads)])

    def seq_swap(a, bits):
        return lax.ppermute(a, "seq", [(i, i ^ bits) for i in range(seqs)])

    def plane_swap(a, dx, dy):
        if dy == 0:
            return head_swap(a, dx * cores)
        if dx == 0:
            return seq_swap(a, dy)
        pairs = [
            (s * heads + h, (s ^ dy) * heads + (h ^ (dx * cores)))
            for s in range(seqs)
            for h in range(heads)
        ]
        return lax.ppermute(a, ("seq", "head"), pairs)

    anywhere = pl.BlockSpec(memory_space=pl.ANY)

    shape = (nx, ny, group, size)
    near = pl.BlockSpec(memory_space=pltpu.VMEM)
    far = pl.BlockSpec(memory_space=pltpu.HBM)

    def call(kernel, out, args, after=(), outs=near, scratch=(), alias={}, fars=()):
        held = [pltpu.with_memory_space_constraint(a, pltpu.VMEM) for a in args]
        there = [pltpu.with_memory_space_constraint(a, pltpu.HBM) for a in fars]
        if outs is near:
            out = jax.tree.map(lambda a: pltpu.VMEM(a.shape, a.dtype), out)
        return pl.pallas_call(
            kernel,
            out_shape=out,
            in_specs=[far] * len(there) + [near] * len(held) + [anywhere] * len(after),
            out_specs=jax.tree.map(lambda _: outs, out),
            scratch_shapes=scratch,
            input_output_aliases=alias,
            compiler_params=pltpu.CompilerParams(vmem_limit_bytes=VMEM),
        )(*there, *held, *after)

    def tie(arrays, after):
        kernel = functools.partial(tie_kernel, len(arrays))
        return call(kernel, [jax.ShapeDtypeStruct(a.shape, a.dtype) for a in arrays], arrays, [after])

    def per_head(a, b):
        return jax.ShapeDtypeStruct((cores * group, a, b), BF16)

    whole = jax.ShapeDtypeStruct((rows, count), BF16)

    dirs, phi_k, phi_w, piece, got, theirs = {}, {}, {}, {}, {}, {}
    near_k, near_q = [], []

    def states(key, after=()):
        half = jax.ShapeDtypeStruct((group // 2 * size, count), BF16)
        rest = jax.ShapeDtypeStruct((rows - half.shape[0], count), BF16)
        outs = [per_head(tokens, count), *([half, rest] if group > 1 else [rest]), whole]
        like = [jax.ShapeDtypeStruct(a.shape, BF16) for a in (k, v, features)]
        if not near_k:
            sems = pltpu.SemaphoreType.DMA((2 * (width // (group * size)) + 1,))
            phi_k[key], *sums, key_block, value_block, part = call(
                functools.partial(first_kernel, key, shape),
                outs + like,
                [near_dirs],
                fars=[k, v, features],
                scratch=[sems],
            )
            near_k.extend([key_block, value_block, part])
        elif not near_q:
            near_k_v_f = [near_k[0], near_k[1], near_k[2], near_dirs]
            phi_k[key], *sums, loaded = call(
                functools.partial(second_kernel, key, shape),
                [*outs, like[0]],
                near_k_v_f,
                fars=[q],
                scratch=[pltpu.SemaphoreType.DMA((1,))],
            )
            near_q.append(loaded)
        else:
            phi_k[key], *sums = call(
                functools.partial(later_kernel, len(after), key, shape),
                outs,
                [*near_k[:2], *directions(key)],
                after,
            )
        *other, mine = sums
        other = [head_swap(a, 1) for a in other]
        theirs[key] = [[other[0], other[-1]], [head_swap(mine, 1)] * 2]
        piece[key] = call(chip_kernel, whole, [mine, *other])
        got[key] = piece[key] if key == (0, 0) else plane_swap(piece[key], *key)
        return mine

    def directions(key):
        return dirs[key] if key[0] != flip else (near_k[2], near_dirs)

    def inner(key, after=()):
        phi_w[key] = call(
            functools.partial(inner_kernel, key, shape),
            [
                per_head(tokens, count),
                jax.ShapeDtypeStruct((cores * group, tokens, 2 * size), F32),
            ],
            [near_q[0], near_k[1], *directions(key), phi_k[key]],
            after,
            scratch=[pltpu.VMEM((cores * group, tokens, tokens), BF16)],
        )
        return phi_w[key][0]

    near_dirs = head_swap(features, 1)
    first = [(flip, dy) for dy in range(ny)]
    later = [(dx, dy) for dx in range(nx) for dy in reversed(range(ny)) if dx != flip]
    for key in first:
        states(key)
    for ox in range(1, nx):
        if ny == 2:
            part = lax.dynamic_slice_in_dim(features, (y ^ 1) * group, group, 0)
            (part,) = tie([head_swap(part, ox * cores)], phi_k[first[-1]])
            rest = seq_swap(part, 1)
            dirs[ox ^ flip, 1] = (part, head_swap(part, 1))
            dirs[ox ^ flip, 0] = (rest, head_swap(rest, 1))
        else:
            (full,) = tie([head_swap(features, ox * cores)], phi_k[first[-1]])
            full = (full, head_swap(full, 1))
            for dy in range(ny):
                dirs[ox ^ flip, dy] = full

    for i, key in enumerate(later):
        states(key, [piece[first[0]] if i == 0 else got[first[0]]])

    summed = call(
        functools.partial(plane_kernel, len(plane), zrows, ny),
        [jax.ShapeDtypeStruct((zrows + TOTAL_ROWS, count), BF16)] * nz,
        [got[key] for key in plane],
        scratch=[pltpu.VMEM((rows, count), F32)],
    )
    heard = [a if j == 0 else seq_swap(a, j * ny) for j, a in enumerate(summed)]
    done = [inner(key, [summed[-1]]) for key in [*first, *later[:-1]]]
    *prefix, totals = call(
        functools.partial(prefix_kernel, nz, zrows, ny),
        [jax.ShapeDtypeStruct((zrows, count), BF16)] * nz
        + [jax.ShapeDtypeStruct((TOTAL_ROWS, count), F32)],
        heard,
        done,
    )
    done = [inner(later[-1], [prefix[-1]])] if later else []
    prefix = [a if j == 0 else seq_swap(a, j * ny) for j, a in enumerate(prefix)]
    placed = call(
        functools.partial(place_kernel, nx, ny, nz, zrows),
        [whole] * len(plane),
        [*prefix, totals, *[got[key] for key in plane]],
        done,
        scratch=[pltpu.VMEM((rows, count), F32)],
    )

    result = {
        key: a if key == (0, 0) else plane_swap(a, *key) for key, a in zip(plane, placed)
    }
    batches = [[((0, 0), 0), ((0, 0), 1)]]
    batches += [[((0, dy), 0)] for dy in range(1, ny)]
    tied = len(batches)
    batches += [[((0, dy), 1)] for dy in range(1, ny)]
    for core in range(cores):
        for dx in range(1, nx):
            batches.append([((dx, dy), core) for dy in range(ny)])
    out = None
    for i, jobs in enumerate(batches):
        args = []
        if i == tied:
            keys = [key for key in plane if key[0]]
            result.update(zip(keys, tie([result[key] for key in keys], out)))
        for key, core in jobs:
            base = head_swap(result[key], 1) if core else result[key]
            args += [*phi_w[key], base, *theirs[key][core]]
        out = call(
            functools.partial(output_kernel, jobs, shape),
            jax.ShapeDtypeStruct((tokens, width), BF16),
            args,
            [] if out is None else [out],
            anywhere,
            [
                pltpu.VMEM((len(jobs), tokens, group * size), BF16),
                pltpu.SemaphoreType.DMA((len(jobs),)),
            ],
            {} if out is None else {len(args): 0},
        )
    return out.reshape(queries.shape)


def solution(mesh):
    token = P(None, ("seq", "head"), None)
    return jax.shard_map(
        functools.partial(body, mesh.shape["seq"], mesh.shape["head"]),
        mesh=mesh,
        in_specs=(token, token, token, P("head", None, None)),
        out_specs=token,
        check_vma=False,
    )
```

```python
import functools
import math

import jax
import jax.numpy as jnp
from jax import lax
from jax.experimental import pallas as pl
from jax.experimental.pallas import tpu as pltpu
from jax.sharding import PartitionSpec as P

F32, BF16 = jnp.float32, jnp.bfloat16
LOG2E = math.log2(math.e)
TOTAL_ROWS = 16
VMEM = 6 * 1024 * 1024


def feature_map(x, w):
    size, count = x.shape[1], w.shape[0]
    c = size ** (-0.25)
    p = lax.dot_general(x, w, (((1,), (1,)), ((), ())), preferred_element_type=F32)
    wide = x.astype(F32)
    square = jnp.sum(wide * wide, axis=1, keepdims=True)
    r = lax.rsqrt(square / size + 1e-06)
    half = square * r * r * (0.5 * c * c * LOG2E) + 0.5 * math.log2(count)
    ww = w.astype(F32)
    ww = ww * ww
    high = ww.astype(BF16)
    low = (ww - high.astype(F32)).astype(BF16)
    ones = jnp.ones((16, size), BF16)
    nt = (((1,), (1,)), ((), ()))
    total = lax.dot_general(ones, high, nt, preferred_element_type=F32)
    total = total + lax.dot_general(ones, low, nt, preferred_element_type=F32)
    s = lax.rsqrt(total[:1] / size + 1e-06)
    return jnp.exp2(p * (r * (c * LOG2E)) * s - half).astype(BF16)


def position(nx, ny):
    head, seq = lax.axis_index("head"), lax.axis_index("seq")
    return head // 2, head % 2, seq % ny, seq // ny


def place_of(pos, key, nx, ny, core):
    flip = 1 if nx > 1 else 0
    part = pos[2] ^ key[1]
    return ((pos[0] ^ key[0] ^ flip) * 2 + (pos[1] ^ core)) * ny + part, part


def heads_of(pos, key, shape, f0, *f1):
    nx, ny, group, size = shape
    for core, fs in ((1, f1), (0, [f0])):
        place, part = place_of(pos, key, nx, ny, core)
        held = sum(f.shape[0] for f in fs)
        first = 0 if held == group else part * group
        for h in range(group):
            start = pl.multiple_of((place * group + h) * size, size)
            f, at = fs[0], first + h
            if len(fs) > 1:
                f, at = fs[h // fs[0].shape[0]], h % fs[0].shape[0]
            yield (1 - core) * group + h, pl.ds(start, size), f, at


def states_kernel(key, shape, waits, k, v, fs, phi, *sums):
    nx, ny, group, size = shape
    *others, mine = sums
    pos = position(nx, ny)
    heads = list(heads_of(pos, key, shape, *fs))
    totals = []
    for i, cols, f, at in heads:
        if i % group == 0:
            waits(i // group)
        ph = feature_map(k[:, cols], f[at])
        phi[i] = ph
        totals.append(jnp.sum(ph.astype(F32), axis=0, keepdims=True))
    waits(2)
    for i, cols, _, _ in heads:
        h, half = i % group, group // 2
        late = i < group and h >= half
        out = mine if i >= group else others[-1] if late else others[0]
        h = h - half if late else h
        st = lax.dot_general(
            v[:, cols], phi[i], (((0,), (0,)), ((), ())), preferred_element_type=F32
        )
        out[h * size : (h + 1) * size] = st.astype(BF16)
    pad = jnp.zeros((TOTAL_ROWS - group, totals[0].shape[1]), F32)
    others[-1][(group - group // 2) * size :] = jnp.concatenate([*totals[:group], pad], axis=0).astype(BF16)
    mine[group * size :] = jnp.concatenate([*totals[group:], pad], axis=0).astype(BF16)
    waits(3)


def first_kernel(key, shape, k_far, v_far, f_far, f1, *refs):
    nx, ny, group, size = shape
    *outs, k, v, f, sems = refs
    wide = group * size
    blocks = k.shape[1] // wide
    place = place_of(position(nx, ny), key, nx, ny, 0)[0]
    copies = [[], [], [], []]

    def fetch(stage, source, target, at):
        copy = pltpu.make_async_copy(source, target, sems.at[at])
        copy.start()
        copies[stage].append(copy)

    def fetch_block(stage, source, target, j, at):
        cols = pl.ds(pl.multiple_of((place ^ j) * wide, wide), wide)
        fetch(stage, source.at[:, cols], target.at[:, cols], at)

    fetch_block(0, k_far, k, ny, 1)
    fetch(1, f_far, f, 0)
    fetch_block(1, k_far, k, 0, 2)
    fetch_block(2, v_far, v, ny, blocks + 1)
    fetch_block(2, v_far, v, 0, blocks + 2)
    rest = [j for j in range(blocks) if j not in (0, ny)]
    for n, j in enumerate(rest):
        fetch_block(3, k_far, k, j, 3 + n)
        fetch_block(3, v_far, v, j, blocks + 3 + n)

    def waits(stage):
        for copy in copies[stage]:
            copy.wait()

    states_kernel(key, shape, waits, k, v, [f, f1], *outs)


def second_kernel(key, shape, q_far, k, v, f0, f1, *refs):
    *outs, q, sem = refs
    copy = pltpu.make_async_copy(q_far, q, sem.at[0])
    copy.start()

    def waits(stage):
        if stage == 3:
            copy.wait()

    states_kernel(key, shape, waits, k, v, [f0, f1], *outs)


def later_kernel(count, extra, key, shape, k, v, *refs):
    fs, outs = refs[:count], refs[count + extra :]
    states_kernel(key, shape, lambda stage: None, k, v, fs, *outs)


def inner_kernel(count, key, shape, q, v, phi_k, *rest):
    phi_q, inner, weights = rest[-3:]
    nx, ny, group, size = shape
    tokens = q.shape[0]
    heads = list(heads_of(position(nx, ny), key, shape, *rest[:count]))
    for i, cols, f, at in heads:
        phi_q[i] = feature_map(q[:, cols], f[at])
    row = lax.broadcasted_iota(jnp.int32, (tokens, tokens), 0)
    col = lax.broadcasted_iota(jnp.int32, (tokens, tokens), 1)
    mask = col <= row
    for i, _, _, _ in heads:
        sc = lax.dot_general(
            phi_q[i], phi_k[i], (((1,), (1,)), ((), ())), preferred_element_type=F32
        )
        weights[i] = jnp.where(mask, sc, 0.0).astype(BF16)
    ones = jnp.ones((tokens, size), BF16)
    for i, cols, _, _ in heads:
        inner[i] = jnp.dot(
            weights[i],
            jnp.concatenate([v[:, cols], ones], axis=1),
            preferred_element_type=F32,
        )


def output_kernel(jobs, shape, extra, *refs):
    out, *marks, ready, sems = refs[5 * len(jobs) + extra :]
    nx, ny, group, size = shape
    pos = position(nx, ny)
    add = (pos[1] == 1).astype(F32)
    copies = []
    for n, (key, core) in enumerate(jobs):
        phi_q, inner, base, extra_a, extra_b = refs[5 * n : 5 * n + 5]
        count = phi_q.shape[-1]
        place = place_of(pos, key, nx, ny, core)[0]
        half = extra_a.shape[0]
        whole = half == base.shape[0]
        last = extra_a[group * size :] if whole else extra_b[group * size - half :]
        totals = base[group * size :].astype(F32) + add * last.astype(F32)
        for h in range(group):
            rows = slice(h * size, (h + 1) * size)
            if whole or h * size < half:
                extra = extra_a[rows]
            else:
                extra = extra_b[h * size - half : (h + 1) * size - half]
            st = (base[rows].astype(F32) + add * extra.astype(F32)).astype(BF16)
            tot = jnp.broadcast_to(totals[h : h + 1], (size, count)).astype(BF16)
            at = (1 - core) * group + h
            acc = inner[at] + lax.dot_general(
                phi_q[at],
                jnp.concatenate([st, tot], axis=0),
                (((1,), (1,)), ((), ())),
                preferred_element_type=F32,
            )
            ready[n, :, rows] = (acc[:, :size] / acc[:, size:]).astype(BF16)
        wide = group * size
        copy = pltpu.make_async_copy(
            ready.at[n],
            out.at[:, pl.ds(pl.multiple_of(place * wide, wide), wide)],
            sems.at[n],
        )
        copy.start()
        copies.append(copy)
    for mark in marks:
        mark[...] = jnp.zeros(mark.shape, F32)
    for copy in copies:
        copy.wait()


def tie_kernel(count, *refs):
    for a, out in zip(refs[:count], refs[-count:]):
        out[...] = a[...]


def chip_kernel(mine, *refs):
    *others, out = refs
    start = 0
    for other in others:
        rows = slice(start, start + other.shape[0])
        start = rows.stop
        out[rows] = (mine[rows].astype(F32) + other[...].astype(F32)).astype(BF16)


def row_kernel(nx, ny, *refs):
    pieces, out, before = refs[:nx], refs[nx], refs[nx + 1 :]
    x = position(nx, ny)[0]
    total = pieces[0][...].astype(F32)
    for piece in pieces[1:]:
        total = total + piece[...].astype(F32)
    out[...] = total.astype(BF16)
    for n, out in enumerate(before):
        total = jnp.zeros(out.shape, F32)
        for ex, piece in enumerate(pieces):
            total = total + jnp.where((x ^ ex) < n + 1, piece[...].astype(F32), 0.0)
        out[...] = total.astype(BF16)


def plane_kernel(count, zrows, ny, *refs):
    held, z = refs[-1], position(1, ny)[3]
    pieces, outs = refs[:count], refs[-1 - (held.shape[0] - TOTAL_ROWS) // zrows : -1]
    total = pieces[0][...].astype(F32)
    for piece in pieces[1:]:
        total = total + piece[...].astype(F32)
    held[...] = total
    srows = len(outs) * zrows
    for j, out in enumerate(outs):
        start = pl.multiple_of((z ^ j) * zrows, zrows)
        out[:zrows] = held[pl.ds(start, zrows)].astype(BF16)
        out[zrows:] = held[srows:].astype(BF16)


def prefix_kernel(count, zrows, ny, *refs):
    heard, outs, totals = refs[count - 1 :: -1], refs[-1 - count : -1], refs[-1]
    z = position(1, ny)[3]
    for j, out in enumerate(outs):
        total = jnp.zeros(out.shape, F32)
        for i, part in enumerate(heard):
            total = total + jnp.where((z ^ i) < (z ^ j), part[:zrows].astype(F32), 0.0)
        out[...] = total.astype(BF16)
    total = jnp.zeros(totals.shape, F32)
    for i, part in enumerate(heard):
        total = total + jnp.where((z ^ i) < z, part[zrows:].astype(F32), 0.0)
    totals[...] = total


def place_kernel(nx, ny, count, zrows, *refs):
    keys = [(dx, dy) for dx in range(nx) for dy in range(ny)]
    prefix, totals = refs[count - 1 :: -1], refs[count]
    row_sums = refs[count + 1 : count + 1 + ny]
    before, outs = refs[count + 1 + ny :], refs[-1 - len(keys) : -1]
    held = refs[-1]
    x, _, y, z = position(nx, ny)
    for j in range(count):
        start = pl.multiple_of((z ^ j) * zrows, zrows)
        held[pl.ds(start, zrows)] = prefix[j][...].astype(F32)
    held[count * zrows :] = totals[...]
    for (dx, dy), out in zip(keys, outs):
        total = held[...]
        for ey, row_sum in enumerate(row_sums):
            total = total + jnp.where((y ^ ey) < (y ^ dy), row_sum[...].astype(F32), 0.0)
        for n in range(nx - 1):
            part = before[dy * (nx - 1) + n][...].astype(F32)
            total = total + jnp.where((x ^ dx) == n + 1, part, 0.0)
        out[...] = total.astype(BF16)


def body(seqs, heads, queries, keys, values, features):
    tokens, width = queries.shape[1:]
    q, k, v = (a.reshape(tokens, width) for a in (queries, keys, values))
    own, count, size = features.shape
    cores = 2
    nx = heads // cores
    ny = nx if seqs % nx == 0 else 1
    nz = seqs // ny
    flip = 1 if nx > 1 else 0
    group = own // ny
    srows = group * size
    zrows = srows // nz
    rows = srows + TOTAL_ROWS
    plane = [(dx, dy) for dx in range(nx) for dy in range(ny)]


    def head_swap(a, bits):
        return lax.ppermute(a, "head", [(i, i ^ bits) for i in range(heads)])

    def seq_swap(a, bits):
        return lax.ppermute(a, "seq", [(i, i ^ bits) for i in range(seqs)])

    def plane_swap(a, dx, dy):
        if dy == 0:
            return head_swap(a, dx * cores)
        if dx == 0:
            return seq_swap(a, dy)
        pairs = [
            (s * heads + h, (s ^ dy) * heads + (h ^ (dx * cores)))
            for s in range(seqs)
            for h in range(heads)
        ]
        return lax.ppermute(a, ("seq", "head"), pairs)

    anywhere = pl.BlockSpec(memory_space=pl.ANY)

    shape = (nx, ny, group, size)
    near = pl.BlockSpec(memory_space=pltpu.VMEM)
    far = pl.BlockSpec(memory_space=pltpu.HBM)

    def call(kernel, out, args, after=(), outs=near, scratch=(), alias={}, fars=()):
        held = [pltpu.with_memory_space_constraint(a, pltpu.VMEM) for a in args]
        there = [pltpu.with_memory_space_constraint(a, pltpu.HBM) for a in fars]
        if outs is near:
            out = jax.tree.map(lambda a: pltpu.VMEM(a.shape, a.dtype), out)
        return pl.pallas_call(
            kernel,
            out_shape=out,
            in_specs=[far] * len(there) + [near] * len(held) + [anywhere] * len(after),
            out_specs=jax.tree.map(lambda _: outs, out) if outs is near else outs,
            scratch_shapes=scratch,
            input_output_aliases=alias,
            compiler_params=pltpu.CompilerParams(vmem_limit_bytes=VMEM),
        )(*there, *held, *after)

    def tie(arrays, after):
        kernel = functools.partial(tie_kernel, len(arrays))
        return call(kernel, [jax.ShapeDtypeStruct(a.shape, a.dtype) for a in arrays], arrays, after)

    def per_head(a, b):
        return jax.ShapeDtypeStruct((cores * group, a, b), BF16)

    whole = jax.ShapeDtypeStruct((rows, count), BF16)

    dirs, phi_k, phi_w, piece, got, theirs = {}, {}, {}, {}, {}, {}
    near_k, near_q = [], []

    def states(key, after=()):
        half = jax.ShapeDtypeStruct((group // 2 * size, count), BF16)
        rest = jax.ShapeDtypeStruct((rows - half.shape[0], count), BF16)
        outs = [per_head(tokens, count), *([half, rest] if group > 1 else [rest]), whole]
        like = [jax.ShapeDtypeStruct(a.shape, BF16) for a in (k, v, features)]
        if not near_k:
            sems = pltpu.SemaphoreType.DMA((2 * (width // (group * size)) + 1,))
            phi_k[key], *sums, key_block, value_block, part = call(
                functools.partial(first_kernel, key, shape),
                outs + like,
                [near_dirs],
                fars=[k, v, features],
                scratch=[sems],
            )
            near_k.extend([key_block, value_block, part])
        elif not near_q:
            near_k_v_f = [near_k[0], near_k[1], near_k[2], near_dirs]
            phi_k[key], *sums, loaded = call(
                functools.partial(second_kernel, key, shape),
                [*outs, like[0]],
                near_k_v_f,
                fars=[q],
                scratch=[pltpu.SemaphoreType.DMA((1,))],
            )
            near_q.append(loaded)
        else:
            phi_k[key], *sums = call(
                functools.partial(later_kernel, len(directions(key)), len(after), key, shape),
                outs,
                [*near_k[:2], *directions(key)],
                after,
            )
        *other, mine = sums
        other = [head_swap(a, 1) for a in other]
        theirs[key] = [[other[0], other[-1]], [head_swap(mine, 1)] * 2]
        piece[key] = call(chip_kernel, whole, [mine, *other])
        got[key] = head_swap(piece[key], key[0] * cores) if key[0] else piece[key]
        return mine

    def directions(key):
        return dirs[key] if key[0] != flip else (near_k[2], near_dirs)

    def inner(key, after=()):
        phi_w[key] = call(
            functools.partial(inner_kernel, len(directions(key)), key, shape),
            [
                per_head(tokens, count),
                jax.ShapeDtypeStruct((cores * group, tokens, 2 * size), F32),
            ],
            [near_q[0], near_k[1], phi_k[key], *directions(key)],
            after,
            scratch=[pltpu.VMEM((cores * group, tokens, tokens), BF16)],
        )
        return phi_w[key][0]

    near_dirs = head_swap(features, 1)
    first = [(flip, dy) for dy in reversed(range(ny))]
    later = [(dx, dy) for dx in range(nx) for dy in reversed(range(ny)) if dx != flip]
    for key in first:
        states(key)
    ready = [piece[first[0]], phi_k[first[-1]]]
    for ox in range(1, nx):
        if ny == 2:
            part = lax.dynamic_slice_in_dim(features, (position(nx, ny)[2] ^ 1) * group, group, 0)
            (part,) = tie([head_swap(part, ox * cores)], ready)
            rest = seq_swap(part, 1)
            dirs[ox ^ flip, 1] = (part, head_swap(part, 1))
            dirs[ox ^ flip, 0] = (rest, head_swap(rest, 1))
        else:
            (full,) = tie([head_swap(features, ox * cores)], ready)
            full = (full, head_swap(full, 1))
            for dy in range(ny):
                dirs[ox ^ flip, dy] = full
    for key in later:
        states(key, [piece[first[0]]])

    rows_of, before = {}, {}
    for dy in reversed(range(ny)):
        sums, *before[dy] = call(
            functools.partial(row_kernel, nx, ny),
            [whole] * nx,
            [got[dx, dy] for dx in range(nx)],
        )
        rows_of[dy] = seq_swap(sums, dy) if dy else sums
    summed = call(
        functools.partial(plane_kernel, ny, zrows, ny),
        [jax.ShapeDtypeStruct((zrows + TOTAL_ROWS, count), BF16)] * nz,
        [rows_of[dy] for dy in range(ny)],
        scratch=[pltpu.VMEM((rows, count), F32)],
    )

    def exchange(parts):
        heard = [seq_swap(parts[j], j * ny) for j in reversed(range(1, nz))]
        return [parts[0], *reversed(heard)]

    heard = exchange(summed)
    done = [inner(key, [summed[-1]]) for key in [*first, *later[:-1]]]
    for dy in range(1, ny):
        before[dy] = [seq_swap(a, dy) for a in tie(before[dy], [summed[0]])] if nx > 1 else []
    *prefix, totals = call(
        functools.partial(prefix_kernel, nz, zrows, ny),
        [jax.ShapeDtypeStruct((zrows, count), BF16)] * nz
        + [jax.ShapeDtypeStruct((TOTAL_ROWS, count), F32)],
        heard[::-1],
        done + [a for dy in range(1, ny) for a in before[dy]],
    )
    done = [inner(later[-1], [prefix[-1]])] if later else []
    prefix = exchange(prefix)
    placed = call(
        functools.partial(place_kernel, nx, ny, nz, zrows),
        [whole] * len(plane),
        [
            *prefix[::-1],
            totals,
            *[rows_of[dy] for dy in range(ny)],
            *[a for dy in range(ny) for a in before[dy]],
        ],
        done,
        scratch=[pltpu.VMEM((rows, count), F32)],
    )

    placed = dict(zip(plane, placed))
    result = {
        key: plane_swap(placed[key], *key) if any(key) else placed[key]
        for key in reversed(plane)
    }
    batches = [[((0, 0), 0), ((0, 0), 1)]]
    batches += [[((0, dy), 0)] for dy in range(1, ny)]
    tied = len(batches)
    batches += [[((0, dy), 1)] for dy in range(1, ny)]
    for core in range(cores):
        for dx in range(1, nx):
            batches.append([((dx, dy), core) for dy in range(ny)])
    out = None
    for i, jobs in enumerate(batches):
        args = []
        if i == tied:
            keys = [key for key in plane if key[0]]
            result.update(zip(keys, tie([result[key] for key in keys], mark)))
        for key, core in jobs:
            base = head_swap(result[key], 1) if core else result[key]
            args += [*phi_w[key], base, *theirs[key][core]]
        marked = [pltpu.VMEM((8, 128), F32)] if i == tied - 1 else []
        out, *mark = call(
            functools.partial(output_kernel, jobs, shape, int(i > 0)),
            [jax.ShapeDtypeStruct((tokens, width), BF16), *marked],
            args,
            [] if out is None else [out],
            [anywhere] + [near] * len(marked),
            [
                pltpu.VMEM((len(jobs), tokens, group * size), BF16),
                pltpu.SemaphoreType.DMA((len(jobs),)),
            ],
            {} if out is None else {len(args): 0},
        )
    return out.reshape(queries.shape)


def solution(mesh):
    token = P(None, ("seq", "head"), None)
    return jax.shard_map(
        functools.partial(body, mesh.shape["seq"], mesh.shape["head"]),
        mesh=mesh,
        in_specs=(token, token, token, P("head", None, None)),
        out_specs=token,
        check_vma=False,
    )
```

```python
import functools
import math

import jax
import jax.numpy as jnp
from jax import lax
from jax.experimental import pallas as pl
from jax.experimental.pallas import tpu as pltpu
from jax.sharding import PartitionSpec as P

F32, BF16 = jnp.float32, jnp.bfloat16
LOG2E = math.log2(math.e)
TOTAL_ROWS = 16
VMEM = 6 * 1024 * 1024


def feature_map(x, w):
    size, count = x.shape[1], w.shape[0]
    c = size ** (-0.25)
    p = lax.dot_general(x, w, (((1,), (1,)), ((), ())), preferred_element_type=F32)
    wide = x.astype(F32)
    square = jnp.sum(wide * wide, axis=1, keepdims=True)
    r = lax.rsqrt(square / size + 1e-06)
    half = square * r * r * (0.5 * c * c * LOG2E) + 0.5 * math.log2(count)
    ww = w.astype(F32)
    ww = ww * ww
    high = ww.astype(BF16)
    low = (ww - high.astype(F32)).astype(BF16)
    ones = jnp.ones((16, size), BF16)
    nt = (((1,), (1,)), ((), ()))
    total = lax.dot_general(ones, high, nt, preferred_element_type=F32)
    total = total + lax.dot_general(ones, low, nt, preferred_element_type=F32)
    s = lax.rsqrt(total[:1] / size + 1e-06)
    return jnp.exp2(p * (r * (c * LOG2E)) * s - half).astype(BF16)


def position(nx, ny):
    head, seq = lax.axis_index("head"), lax.axis_index("seq")
    return head // 2, head % 2, seq % ny, seq // ny


def place_of(pos, key, nx, ny, core):
    flip = 1 if nx > 1 else 0
    part = pos[2] ^ key[1]
    return ((pos[0] ^ key[0] ^ flip) * 2 + (pos[1] ^ core)) * ny + part, part


def heads_of(pos, key, shape, f0, *f1):
    nx, ny, group, size = shape
    for core, fs in ((1, f1), (0, [f0])):
        place, part = place_of(pos, key, nx, ny, core)
        held = sum(f.shape[0] for f in fs)
        first = 0 if held == group else part * group
        for h in range(group):
            start = pl.multiple_of((place * group + h) * size, size)
            f, at = fs[0], first + h
            if len(fs) > 1:
                f, at = fs[h // fs[0].shape[0]], h % fs[0].shape[0]
            yield (1 - core) * group + h, pl.ds(start, size), f, at


def states_kernel(key, shape, waits, k, v, fs, phi, *sums):
    nx, ny, group, size = shape
    *others, mine = sums
    pos = position(nx, ny)
    heads = list(heads_of(pos, key, shape, *fs))
    totals = []
    for i, cols, f, at in heads:
        if i % group == 0:
            waits(i // group)
        ph = feature_map(k[:, cols], f[at])
        phi[i] = ph
        totals.append(jnp.sum(ph.astype(F32), axis=0, keepdims=True))
    waits(2)
    for i, cols, _, _ in heads:
        h, out, each = i % group, mine, group // len(others)
        if i < group:
            h, out = h % each, others[h // each]
        st = lax.dot_general(
            v[:, cols], phi[i], (((0,), (0,)), ((), ())), preferred_element_type=F32
        )
        out[h * size : (h + 1) * size] = st.astype(BF16)
    pad = jnp.zeros((TOTAL_ROWS - group, totals[0].shape[1]), F32)
    others[-1][group // len(others) * size :] = jnp.concatenate([*totals[:group], pad], axis=0).astype(BF16)
    mine[group * size :] = jnp.concatenate([*totals[group:], pad], axis=0).astype(BF16)
    waits(3)


def first_kernel(key, shape, k_far, v_far, f_far, f1, *refs):
    nx, ny, group, size = shape
    *outs, k, v, f, sems = refs
    wide = group * size
    blocks = k.shape[1] // wide
    place = place_of(position(nx, ny), key, nx, ny, 0)[0]
    copies = [[], [], [], []]

    def fetch(stage, source, target, at):
        copy = pltpu.make_async_copy(source, target, sems.at[at])
        copy.start()
        copies[stage].append(copy)

    def fetch_block(stage, source, target, j, at):
        cols = pl.ds(pl.multiple_of((place ^ j) * wide, wide), wide)
        fetch(stage, source.at[:, cols], target.at[:, cols], at)

    fetch_block(0, k_far, k, ny, 1)
    fetch(1, f_far, f, 0)
    fetch_block(1, k_far, k, 0, 2)
    fetch_block(2, v_far, v, ny, blocks + 1)
    fetch_block(2, v_far, v, 0, blocks + 2)
    rest = [j for j in range(blocks) if j not in (0, ny)]
    for n, j in enumerate(rest):
        fetch_block(3, k_far, k, j, 3 + n)
        fetch_block(3, v_far, v, j, blocks + 3 + n)

    def waits(stage):
        for copy in copies[stage]:
            copy.wait()

    states_kernel(key, shape, waits, k, v, [f, f1], *outs)


def second_kernel(key, shape, q_far, k, v, f0, f1, *refs):
    *outs, q, sem = refs
    copy = pltpu.make_async_copy(q_far, q, sem.at[0])
    copy.start()

    def waits(stage):
        if stage == 3:
            copy.wait()

    states_kernel(key, shape, waits, k, v, [f0, f1], *outs)


def later_kernel(count, extra, key, shape, k, v, *refs):
    fs, outs = refs[:count], refs[count + extra :]
    states_kernel(key, shape, lambda stage: None, k, v, fs, *outs)


def inner_kernel(count, key, shape, q, v, phi_k, *rest):
    phi_q, inner, weights = rest[-3:]
    nx, ny, group, size = shape
    tokens = q.shape[0]
    heads = list(heads_of(position(nx, ny), key, shape, *rest[:count]))
    for i, cols, f, at in heads:
        phi_q[i] = feature_map(q[:, cols], f[at])
    row = lax.broadcasted_iota(jnp.int32, (tokens, tokens), 0)
    col = lax.broadcasted_iota(jnp.int32, (tokens, tokens), 1)
    mask = col <= row
    for i, _, _, _ in heads:
        sc = lax.dot_general(
            phi_q[i], phi_k[i], (((1,), (1,)), ((), ())), preferred_element_type=F32
        )
        weights[i] = jnp.where(mask, sc, 0.0).astype(BF16)
    ones = jnp.ones((tokens, size), BF16)
    for i, cols, _, _ in heads:
        inner[i] = jnp.dot(
            weights[i],
            jnp.concatenate([v[:, cols], ones], axis=1),
            preferred_element_type=F32,
        )


def output_kernel(jobs, counts, shape, extra, *refs):
    jobs_refs, at = [], 0
    for count in counts:
        jobs_refs.append(refs[at : at + count])
        at += count
    out, *marks, ready, sems = refs[at + extra :]
    nx, ny, group, size = shape
    pos = position(nx, ny)
    add = (pos[1] == 1).astype(F32)
    copies = []
    for n, (key, core) in enumerate(jobs):
        phi_q, inner, base, *extras = jobs_refs[n]
        count = phi_q.shape[-1]
        place = place_of(pos, key, nx, ny, core)[0]
        each = group // len(extras)
        last = extras[-1][each * size :]
        totals = base[group * size :].astype(F32) + add * last.astype(F32)
        for h in range(group):
            rows = slice(h * size, (h + 1) * size)
            extra = extras[h // each][h % each * size : (h % each + 1) * size]
            st = (base[rows].astype(F32) + add * extra.astype(F32)).astype(BF16)
            tot = jnp.broadcast_to(totals[h : h + 1], (size, count)).astype(BF16)
            at = (1 - core) * group + h
            acc = inner[at] + lax.dot_general(
                phi_q[at],
                jnp.concatenate([st, tot], axis=0),
                (((1,), (1,)), ((), ())),
                preferred_element_type=F32,
            )
            ready[n, :, rows] = (acc[:, :size] / acc[:, size:]).astype(BF16)
        wide = group * size
        copy = pltpu.make_async_copy(
            ready.at[n],
            out.at[:, pl.ds(pl.multiple_of(place * wide, wide), wide)],
            sems.at[n],
        )
        copy.start()
        copies.append(copy)
    for mark in marks:
        mark[...] = jnp.zeros(mark.shape, F32)
    for copy in copies:
        copy.wait()


def tie_kernel(count, *refs):
    for a, out in zip(refs[:count], refs[-count:]):
        out[...] = a[...]


def chip_kernel(mine, *refs):
    *others, out = refs
    start = 0
    for other in others:
        rows = slice(start, start + other.shape[0])
        start = rows.stop
        out[rows] = (mine[rows].astype(F32) + other[...].astype(F32)).astype(BF16)


def row_kernel(*refs):
    *pieces, out = refs
    total = pieces[0][...].astype(F32)
    for piece in pieces[1:]:
        total = total + piece[...].astype(F32)
    out[...] = total.astype(BF16)


def plane_kernel(count, zrows, ny, *refs):
    held, z = refs[-1], position(1, ny)[3]
    pieces, outs = refs[:count], refs[-1 - (held.shape[0] - TOTAL_ROWS) // zrows : -1]
    total = pieces[0][...].astype(F32)
    for piece in pieces[1:]:
        total = total + piece[...].astype(F32)
    held[...] = total
    srows = len(outs) * zrows
    for j, out in enumerate(outs):
        start = pl.multiple_of((z ^ j) * zrows, zrows)
        out[:zrows] = held[pl.ds(start, zrows)].astype(BF16)
        out[zrows:] = held[srows:].astype(BF16)


def prefix_kernel(count, zrows, ny, *refs):
    heard, outs, totals = refs[count - 1 :: -1], refs[-1 - count : -1], refs[-1]
    z = position(1, ny)[3]
    for j, out in enumerate(outs):
        total = jnp.zeros(out.shape, F32)
        for i, part in enumerate(heard):
            total = total + jnp.where((z ^ i) < (z ^ j), part[:zrows].astype(F32), 0.0)
        out[...] = total.astype(BF16)
    total = jnp.zeros(totals.shape, F32)
    for i, part in enumerate(heard):
        total = total + jnp.where((z ^ i) < z, part[zrows:].astype(F32), 0.0)
    totals[...] = total


def rows_kernel(ny, count, zrows, *refs):
    prefix, totals = refs[count - 1 :: -1], refs[count]
    row_sums, outs, held = refs[count + 1 : count + 1 + ny], refs[-1 - ny : -1], refs[-1]
    _, _, y, z = position(1, ny)
    for j in range(count):
        start = pl.multiple_of((z ^ j) * zrows, zrows)
        held[pl.ds(start, zrows)] = prefix[j][...].astype(F32)
    held[count * zrows :] = totals[...]
    for dy, out in enumerate(outs):
        total = held[...]
        for ey, row_sum in enumerate(row_sums):
            if ey != dy:
                total = total + jnp.where((y ^ ey) < (y ^ dy), row_sum[...].astype(F32), 0.0)
        out[...] = total.astype(out.dtype)


def columns_kernel(nx, ny, base, *refs):
    pieces, outs = refs[:nx], refs[nx:]
    x = position(nx, ny)[0]
    for dx, out in enumerate(outs):
        total = base[...].astype(F32)
        for ex, piece in enumerate(pieces):
            if ex != dx:
                total = total + jnp.where((x ^ ex) < (x ^ dx), piece[...].astype(F32), 0.0)
        out[...] = total.astype(BF16)


def body(seqs, heads, queries, keys, values, features):
    tokens, width = queries.shape[1:]
    q, k, v = (a.reshape(tokens, width) for a in (queries, keys, values))
    own, count, size = features.shape
    cores = 2
    nx = heads // cores
    ny = nx if seqs % nx == 0 else 1
    nz = seqs // ny
    flip = 1 if nx > 1 else 0
    group = own // ny
    srows = group * size
    zrows = srows // nz
    rows = srows + TOTAL_ROWS
    plane = [(dx, dy) for dx in range(nx) for dy in range(ny)]


    def head_swap(a, bits):
        return lax.ppermute(a, "head", [(i, i ^ bits) for i in range(heads)])

    def seq_swap(a, bits):
        return lax.ppermute(a, "seq", [(i, i ^ bits) for i in range(seqs)])

    def plane_swap(a, dx, dy):
        if dy == 0:
            return head_swap(a, dx * cores)
        if dx == 0:
            return seq_swap(a, dy)
        pairs = [
            (s * heads + h, (s ^ dy) * heads + (h ^ (dx * cores)))
            for s in range(seqs)
            for h in range(heads)
        ]
        return lax.ppermute(a, ("seq", "head"), pairs)

    anywhere = pl.BlockSpec(memory_space=pl.ANY)

    shape = (nx, ny, group, size)
    near = pl.BlockSpec(memory_space=pltpu.VMEM)
    far = pl.BlockSpec(memory_space=pltpu.HBM)

    def call(kernel, out, args, after=(), outs=near, scratch=(), alias={}, fars=()):
        held = [pltpu.with_memory_space_constraint(a, pltpu.VMEM) for a in args]
        there = [pltpu.with_memory_space_constraint(a, pltpu.HBM) for a in fars]
        if outs is near:
            out = jax.tree.map(lambda a: pltpu.VMEM(a.shape, a.dtype), out)
        return pl.pallas_call(
            kernel,
            out_shape=out,
            in_specs=[far] * len(there) + [near] * len(held) + [anywhere] * len(after),
            out_specs=jax.tree.map(lambda _: outs, out) if outs is near else outs,
            scratch_shapes=scratch,
            input_output_aliases=alias,
            compiler_params=pltpu.CompilerParams(vmem_limit_bytes=VMEM),
        )(*there, *held, *after)

    def tie(arrays, after):
        kernel = functools.partial(tie_kernel, len(arrays))
        return call(kernel, [jax.ShapeDtypeStruct(a.shape, a.dtype) for a in arrays], arrays, after)

    def per_head(a, b):
        return jax.ShapeDtypeStruct((cores * group, a, b), BF16)

    whole = jax.ShapeDtypeStruct((rows, count), BF16)

    dirs, phi_k, phi_w, piece, got, theirs = {}, {}, {}, {}, {}, {}
    near_k, near_q = [], []

    def states(key, after=()):
        cuts = group if key == later[0] else min(group, 2)
        cut = [group // cuts * size] * cuts
        cut[-1] += TOTAL_ROWS
        cut = [jax.ShapeDtypeStruct((n, count), BF16) for n in cut]
        outs = [per_head(tokens, count), *cut, whole]
        like = [jax.ShapeDtypeStruct(a.shape, BF16) for a in (k, v, features)]
        if not near_k:
            sems = pltpu.SemaphoreType.DMA((2 * (width // (group * size)) + 1,))
            phi_k[key], *sums, key_block, value_block, part = call(
                functools.partial(first_kernel, key, shape),
                outs + like,
                [near_dirs],
                fars=[k, v, features],
                scratch=[sems],
            )
            near_k.extend([key_block, value_block, part])
        elif not near_q:
            near_k_v_f = [near_k[0], near_k[1], near_k[2], near_dirs]
            phi_k[key], *sums, loaded = call(
                functools.partial(second_kernel, key, shape),
                [*outs, like[0]],
                near_k_v_f,
                fars=[q],
                scratch=[pltpu.SemaphoreType.DMA((1,))],
            )
            near_q.append(loaded)
        else:
            phi_k[key], *sums = call(
                functools.partial(later_kernel, len(directions(key)), len(after), key, shape),
                outs,
                [*near_k[:2], *directions(key)],
                after,
            )
        *other, mine = sums
        other = [head_swap(a, 1) for a in other]
        theirs[key] = [other, [head_swap(mine, 1)]]
        piece[key] = call(chip_kernel, whole, [mine, *other])
        got[key] = head_swap(piece[key], key[0] * cores) if key[0] else piece[key]
        return mine

    def directions(key):
        return dirs[key] if key[0] != flip else (near_k[2], near_dirs)

    def inner(key, after=()):
        phi_w[key] = call(
            functools.partial(inner_kernel, len(directions(key)), key, shape),
            [
                per_head(tokens, count),
                jax.ShapeDtypeStruct((cores * group, tokens, 2 * size), F32),
            ],
            [near_q[0], near_k[1], phi_k[key], *directions(key)],
            after,
            scratch=[pltpu.VMEM((cores * group, tokens, tokens), BF16)],
        )
        return phi_w[key][0]

    near_dirs = head_swap(features, 1)
    first = [(flip, dy) for dy in reversed(range(ny))]
    later = [(dx, dy) for dx in range(nx) for dy in reversed(range(ny)) if dx != flip]
    for key in first:
        states(key)
    ready = [piece[first[0]], phi_k[first[-1]]]
    for ox in range(1, nx):
        if ny == 2:
            part = lax.dynamic_slice_in_dim(features, (position(nx, ny)[2] ^ 1) * group, group, 0)
            (part,) = tie([head_swap(part, ox * cores)], ready)
            rest = seq_swap(part, 1)
            dirs[ox ^ flip, 1] = (part, head_swap(part, 1))
            dirs[ox ^ flip, 0] = (rest,)
        else:
            (full,) = tie([head_swap(features, ox * cores)], ready)
            full = (full, head_swap(full, 1))
            for dy in range(ny):
                dirs[ox ^ flip, dy] = full
    for key in later:
        if key != later[0] and ny == 2:
            (rest,) = tie([dirs[key][0]], [piece[later[0]]])
            dirs[key] = (rest, head_swap(rest, 1))
        states(key, [piece[key] for key in first])

    rows_of = {}
    for dy in reversed(range(ny)):
        sums = call(row_kernel, whole, [got[dx, dy] for dx in range(nx)])
        rows_of[dy] = seq_swap(sums, dy) if dy else sums
    summed = call(
        functools.partial(plane_kernel, ny, zrows, ny),
        [jax.ShapeDtypeStruct((zrows + TOTAL_ROWS, count), BF16)] * nz,
        [rows_of[dy] for dy in range(ny)],
        scratch=[pltpu.VMEM((rows, count), F32)],
    )

    def exchange(parts):
        heard = [seq_swap(parts[j], j * ny) for j in reversed(range(1, nz))]
        return [parts[0], *reversed(heard)]

    heard = exchange(summed)
    done = [inner(key, [summed[-1]]) for key in [*first, *later[:-1]]]
    *prefix, totals = call(
        functools.partial(prefix_kernel, nz, zrows, ny),
        [jax.ShapeDtypeStruct((zrows, count), BF16)] * nz
        + [jax.ShapeDtypeStruct((TOTAL_ROWS, count), F32)],
        heard[::-1],
        done,
    )
    done = [inner(later[-1], [prefix[-1]])] if later else []
    prefix = exchange(prefix)
    bases = call(
        functools.partial(rows_kernel, ny, nz, zrows),
        [jax.ShapeDtypeStruct((rows, count), BF16 if dy else F32) for dy in range(ny)],
        [*prefix[::-1], totals, *[rows_of[dy] for dy in range(ny)]],
        done,
        scratch=[pltpu.VMEM((rows, count), F32)],
    )
    result = {}
    for dy, base in enumerate(bases):
        placed = call(
            functools.partial(columns_kernel, nx, ny),
            [whole] * nx,
            [seq_swap(base, dy) if dy else base, *[got[dx, dy] for dx in range(nx)]],
        )
        for dx, a in enumerate(placed):
            result[dx, dy] = head_swap(a, dx * cores) if dx else a

    late = [key for key in plane if all(key)]
    soon = [key for key in plane if not key[0]]
    batches = [[(key, 0), (key, 1)] for key in soon]
    tied = len(batches)
    batches += [[(key, 0) for key in late]] if late else []
    batches += [[(key, 0), (key, 1)] for key in plane if key not in late + soon]
    batches += [[(key, 1) for key in late]] if late else []
    out = None
    for i, jobs in enumerate(batches):
        args = []
        if i == tied:
            result.update(zip(late, tie([result[key] for key in late], mark)))
        counts = []
        for key, core in jobs:
            base = head_swap(result[key], 1) if core else result[key]
            args += [*phi_w[key], base, *theirs[key][core]]
            counts.append(3 + len(theirs[key][core]))
        marked = [pltpu.VMEM((8, 128), F32)] if i == tied - 1 else []
        out, *mark = call(
            functools.partial(output_kernel, jobs, counts, shape, int(i > 0)),
            [jax.ShapeDtypeStruct((tokens, width), BF16), *marked],
            args,
            [] if out is None else [out],
            [anywhere] + [near] * len(marked),
            [
                pltpu.VMEM((len(jobs), tokens, group * size), BF16),
                pltpu.SemaphoreType.DMA((len(jobs),)),
            ],
            {} if out is None else {len(args): 0},
        )
    return out.reshape(queries.shape)


def solution(mesh):
    token = P(None, ("seq", "head"), None)
    return jax.shard_map(
        functools.partial(body, mesh.shape["seq"], mesh.shape["head"]),
        mesh=mesh,
        in_specs=(token, token, token, P("head", None, None)),
        out_specs=token,
        check_vma=False,
    )
```

```python
import functools
import math

import jax
import jax.numpy as jnp
from jax import lax
from jax.experimental import pallas as pl
from jax.experimental.pallas import tpu as pltpu
from jax.sharding import PartitionSpec as P

F32, BF16 = jnp.float32, jnp.bfloat16
LOG2E = math.log2(math.e)
TOTAL_ROWS = 16
VMEM = 6 * 1024 * 1024


def feature_map(x, w):
    size, count = x.shape[1], w.shape[0]
    c = size ** (-0.25)
    p = lax.dot_general(x, w, (((1,), (1,)), ((), ())), preferred_element_type=F32)
    wide = x.astype(F32)
    square = jnp.sum(wide * wide, axis=1, keepdims=True)
    r = lax.rsqrt(square / size + 1e-06)
    half = square * r * r * (0.5 * c * c * LOG2E) + 0.5 * math.log2(count)
    ww = w.astype(F32)
    ww = ww * ww
    high = ww.astype(BF16)
    low = (ww - high.astype(F32)).astype(BF16)
    ones = jnp.ones((16, size), BF16)
    nt = (((1,), (1,)), ((), ()))
    total = lax.dot_general(ones, high, nt, preferred_element_type=F32)
    total = total + lax.dot_general(ones, low, nt, preferred_element_type=F32)
    s = lax.rsqrt(total[:1] / size + 1e-06)
    return jnp.exp2(p * (r * (c * LOG2E)) * s - half).astype(BF16)


def position(nx, ny):
    head, seq = lax.axis_index("head"), lax.axis_index("seq")
    return head // 2, head % 2, seq % ny, seq // ny


def place_of(pos, key, nx, ny, core):
    flip = 1 if nx > 1 else 0
    part = pos[2] ^ key[1]
    return ((pos[0] ^ key[0] ^ flip) * 2 + (pos[1] ^ core)) * ny + part, part


def heads_of(pos, key, shape, f0, *f1):
    nx, ny, group, size = shape
    for core, fs in ((1, f1), (0, [f0])):
        place, part = place_of(pos, key, nx, ny, core)
        held = sum(f.shape[0] for f in fs)
        first = 0 if held == group else part * group
        for h in range(group):
            start = pl.multiple_of((place * group + h) * size, size)
            f, at = fs[0], first + h
            if len(fs) > 1:
                f, at = fs[h // fs[0].shape[0]], h % fs[0].shape[0]
            yield (1 - core) * group + h, pl.ds(start, size), f, at


def states_kernel(key, shape, waits, k, v, fs, phi, *sums):
    nx, ny, group, size = shape
    *others, mine = sums
    pos = position(nx, ny)
    heads = list(heads_of(pos, key, shape, *fs))
    totals = []
    for i, cols, f, at in heads:
        if i % group == 0:
            waits(i // group)
        ph = feature_map(k[:, cols], f[at])
        phi[i] = ph
        totals.append(jnp.sum(ph.astype(F32), axis=0, keepdims=True))
    waits(2)
    for i, cols, _, _ in heads:
        h, out, each = i % group, mine, group // len(others)
        if i < group:
            h, out = h % each, others[h // each]
        st = lax.dot_general(
            v[:, cols], phi[i], (((0,), (0,)), ((), ())), preferred_element_type=F32
        )
        out[h * size : (h + 1) * size] = st.astype(BF16)
    pad = jnp.zeros((TOTAL_ROWS - group, totals[0].shape[1]), F32)
    others[-1][group // len(others) * size :] = jnp.concatenate([*totals[:group], pad], axis=0).astype(BF16)
    mine[group * size :] = jnp.concatenate([*totals[group:], pad], axis=0).astype(BF16)
    waits(3)


def first_kernel(key, shape, k_far, v_far, f_far, f1, *refs):
    nx, ny, group, size = shape
    *outs, k, v, f, sems = refs
    wide = group * size
    blocks = k.shape[1] // wide
    place = place_of(position(nx, ny), key, nx, ny, 0)[0]
    copies = [[], [], [], []]

    def fetch(stage, source, target, at):
        copy = pltpu.make_async_copy(source, target, sems.at[at])
        copy.start()
        copies[stage].append(copy)

    def fetch_block(stage, source, target, j, at):
        cols = pl.ds(pl.multiple_of((place ^ j) * wide, wide), wide)
        fetch(stage, source.at[:, cols], target.at[:, cols], at)

    fetch_block(0, k_far, k, ny, 1)
    fetch(1, f_far, f, 0)
    fetch_block(1, k_far, k, 0, 2)
    fetch_block(2, v_far, v, ny, blocks + 1)
    fetch_block(2, v_far, v, 0, blocks + 2)
    rest = [j for j in range(blocks) if j not in (0, ny)]
    for n, j in enumerate(rest):
        fetch_block(3, k_far, k, j, 3 + n)
        fetch_block(3, v_far, v, j, blocks + 3 + n)

    def waits(stage):
        for copy in copies[stage]:
            copy.wait()

    states_kernel(key, shape, waits, k, v, [f, f1], *outs)


def second_kernel(key, shape, q_far, k, v, f0, f1, *refs):
    *outs, q, sem = refs
    copy = pltpu.make_async_copy(q_far, q, sem.at[0])
    copy.start()

    def waits(stage):
        if stage == 3:
            copy.wait()

    states_kernel(key, shape, waits, k, v, [f0, f1], *outs)


def later_kernel(count, extra, key, shape, k, v, *refs):
    fs, outs = refs[:count], refs[count + extra :]
    states_kernel(key, shape, lambda stage: None, k, v, fs, *outs)


def inner_kernel(count, key, shape, q, v, phi_k, *rest):
    phi_q, inner, weights = rest[-3:]
    nx, ny, group, size = shape
    tokens = q.shape[0]
    heads = list(heads_of(position(nx, ny), key, shape, *rest[:count]))
    for i, cols, f, at in heads:
        phi_q[i] = feature_map(q[:, cols], f[at])
    row = lax.broadcasted_iota(jnp.int32, (tokens, tokens), 0)
    col = lax.broadcasted_iota(jnp.int32, (tokens, tokens), 1)
    mask = col <= row
    for i, _, _, _ in heads:
        sc = lax.dot_general(
            phi_q[i], phi_k[i], (((1,), (1,)), ((), ())), preferred_element_type=F32
        )
        weights[i] = jnp.where(mask, sc, 0.0).astype(BF16)
    ones = jnp.ones((tokens, size), BF16)
    for i, cols, _, _ in heads:
        inner[i] = jnp.dot(
            weights[i],
            jnp.concatenate([v[:, cols], ones], axis=1),
            preferred_element_type=F32,
        )


def output_kernel(jobs, counts, shape, extra, *refs):
    jobs_refs, at = [], 0
    for count in counts:
        jobs_refs.append(refs[at : at + count])
        at += count
    out, *marks, ready, sems = refs[at + extra :]
    nx, ny, group, size = shape
    pos = position(nx, ny)
    add = (pos[1] == 1).astype(F32)
    copies = []
    for n, (key, core) in enumerate(jobs):
        phi_q, inner, base, *extras = jobs_refs[n]
        count = phi_q.shape[-1]
        place = place_of(pos, key, nx, ny, core)[0]
        each = group // max(len(extras), 1)
        totals = base[group * size :].astype(F32)
        if extras:
            totals = totals + add * extras[-1][each * size :].astype(F32)
        for h in range(group):
            rows = slice(h * size, (h + 1) * size)
            st = base[rows]
            if extras:
                extra = extras[h // each][h % each * size : (h % each + 1) * size]
                st = (st.astype(F32) + add * extra.astype(F32)).astype(BF16)
            tot = jnp.broadcast_to(totals[h : h + 1], (size, count)).astype(BF16)
            at = (1 - core) * group + h
            acc = inner[at] + lax.dot_general(
                phi_q[at],
                jnp.concatenate([st, tot], axis=0),
                (((1,), (1,)), ((), ())),
                preferred_element_type=F32,
            )
            ready[n, :, rows] = (acc[:, :size] / acc[:, size:]).astype(BF16)
            start = pl.multiple_of((place * group + h) * size, size)
            copy = pltpu.make_async_copy(
                ready.at[n, :, rows], out.at[:, pl.ds(start, size)], sems.at[n, h]
            )
            copy.start()
            copies.append(copy)
    for mark in marks:
        mark[...] = jnp.zeros(mark.shape, F32)
    for copy in copies:
        copy.wait()


def far_kernel(shape, base, mine, *refs):
    add = (position(*shape[:2])[1] == 0).astype(F32)
    refs[-1][...] = (base[...].astype(F32) + add * mine[...].astype(F32)).astype(BF16)


def tie_kernel(count, *refs):
    for a, out in zip(refs[:count], refs[-count:]):
        out[...] = a[...]


def chip_kernel(mine, *refs):
    *others, out = refs
    start = 0
    for other in others:
        rows = slice(start, start + other.shape[0])
        start = rows.stop
        out[rows] = (mine[rows].astype(F32) + other[...].astype(F32)).astype(BF16)


def row_kernel(*refs):
    *pieces, out = refs
    total = pieces[0][...].astype(F32)
    for piece in pieces[1:]:
        total = total + piece[...].astype(F32)
    out[...] = total.astype(BF16)


def plane_kernel(count, zrows, ny, *refs):
    held, z = refs[-1], position(1, ny)[3]
    pieces, outs = refs[:count], refs[-1 - (held.shape[0] - TOTAL_ROWS) // zrows : -1]
    total = pieces[0][...].astype(F32)
    for piece in pieces[1:]:
        total = total + piece[...].astype(F32)
    held[...] = total
    srows = len(outs) * zrows
    for j, out in enumerate(outs):
        start = pl.multiple_of((z ^ j) * zrows, zrows)
        out[:zrows] = held[pl.ds(start, zrows)].astype(BF16)
        out[zrows:] = held[srows:].astype(BF16)


def prefix_kernel(count, zrows, ny, *refs):
    heard, outs, totals = refs[count - 1 :: -1], refs[-1 - count : -1], refs[-1]
    z = position(1, ny)[3]
    for j, out in enumerate(outs):
        total = jnp.zeros(out.shape, F32)
        for i, part in enumerate(heard):
            total = total + jnp.where((z ^ i) < (z ^ j), part[:zrows].astype(F32), 0.0)
        out[...] = total.astype(BF16)
    total = jnp.zeros(totals.shape, F32)
    for i, part in enumerate(heard):
        total = total + jnp.where((z ^ i) < z, part[zrows:].astype(F32), 0.0)
    totals[...] = total


def rows_kernel(ny, count, zrows, *refs):
    prefix, totals = refs[count - 1 :: -1], refs[count]
    row_sums, outs, held = refs[count + 1 : count + 1 + ny], refs[-1 - ny : -1], refs[-1]
    _, _, y, z = position(1, ny)
    for j in range(count):
        start = pl.multiple_of((z ^ j) * zrows, zrows)
        held[pl.ds(start, zrows)] = prefix[j][...].astype(F32)
    held[count * zrows :] = totals[...]
    for dy, out in enumerate(outs):
        total = held[...]
        for ey, row_sum in enumerate(row_sums):
            if ey != dy:
                total = total + jnp.where((y ^ ey) < (y ^ dy), row_sum[...].astype(F32), 0.0)
        out[...] = total.astype(out.dtype)


def columns_kernel(nx, ny, base, *refs):
    pieces, outs = refs[:nx], refs[nx:]
    x = position(nx, ny)[0]
    for dx, out in enumerate(outs):
        total = base[...].astype(F32)
        for ex, piece in enumerate(pieces):
            if ex != dx:
                total = total + jnp.where((x ^ ex) < (x ^ dx), piece[...].astype(F32), 0.0)
        out[...] = total.astype(BF16)


def body(seqs, heads, queries, keys, values, features):
    tokens, width = queries.shape[1:]
    q, k, v = (a.reshape(tokens, width) for a in (queries, keys, values))
    own, count, size = features.shape
    cores = 2
    nx = heads // cores
    ny = nx if seqs % nx == 0 else 1
    nz = seqs // ny
    flip = 1 if nx > 1 else 0
    group = own // ny
    srows = group * size
    zrows = srows // nz
    rows = srows + TOTAL_ROWS
    plane = [(dx, dy) for dx in range(nx) for dy in range(ny)]


    def head_swap(a, bits):
        return lax.ppermute(a, "head", [(i, i ^ bits) for i in range(heads)])

    def seq_swap(a, bits):
        return lax.ppermute(a, "seq", [(i, i ^ bits) for i in range(seqs)])

    def plane_swap(a, dx, dy):
        if dy == 0:
            return head_swap(a, dx * cores)
        if dx == 0:
            return seq_swap(a, dy)
        pairs = [
            (s * heads + h, (s ^ dy) * heads + (h ^ (dx * cores)))
            for s in range(seqs)
            for h in range(heads)
        ]
        return lax.ppermute(a, ("seq", "head"), pairs)

    anywhere = pl.BlockSpec(memory_space=pl.ANY)

    shape = (nx, ny, group, size)
    near = pl.BlockSpec(memory_space=pltpu.VMEM)
    far = pl.BlockSpec(memory_space=pltpu.HBM)

    def call(kernel, out, args, after=(), outs=near, scratch=(), alias={}, fars=()):
        held = [pltpu.with_memory_space_constraint(a, pltpu.VMEM) for a in args]
        there = [pltpu.with_memory_space_constraint(a, pltpu.HBM) for a in fars]
        if outs is near:
            out = jax.tree.map(lambda a: pltpu.VMEM(a.shape, a.dtype), out)
        return pl.pallas_call(
            kernel,
            out_shape=out,
            in_specs=[far] * len(there) + [near] * len(held) + [anywhere] * len(after),
            out_specs=jax.tree.map(lambda _: outs, out) if outs is near else outs,
            scratch_shapes=scratch,
            input_output_aliases=alias,
            compiler_params=pltpu.CompilerParams(vmem_limit_bytes=VMEM),
        )(*there, *held, *after)

    def tie(arrays, after):
        kernel = functools.partial(tie_kernel, len(arrays))
        return call(kernel, [jax.ShapeDtypeStruct(a.shape, a.dtype) for a in arrays], arrays, after)

    def per_head(a, b):
        return jax.ShapeDtypeStruct((cores * group, a, b), BF16)

    whole = jax.ShapeDtypeStruct((rows, count), BF16)

    dirs, phi_k, phi_w, piece, got, theirs = {}, {}, {}, {}, {}, {}
    near_k, near_q, own_sums = [], [], {}

    def states(key, after=()):
        cuts = group if key == later[0] else min(group, 2)
        cut = [group // cuts * size] * cuts
        cut[-1] += TOTAL_ROWS
        cut = [jax.ShapeDtypeStruct((n, count), BF16) for n in cut]
        outs = [per_head(tokens, count), *cut, whole]
        like = [jax.ShapeDtypeStruct(a.shape, BF16) for a in (k, v, features)]
        if not near_k:
            sems = pltpu.SemaphoreType.DMA((2 * (width // (group * size)) + 1,))
            phi_k[key], *sums, key_block, value_block, part = call(
                functools.partial(first_kernel, key, shape),
                outs + like,
                [near_dirs],
                fars=[k, v, features],
                scratch=[sems],
            )
            near_k.extend([key_block, value_block, part])
        elif not near_q:
            near_k_v_f = [near_k[0], near_k[1], near_k[2], near_dirs]
            phi_k[key], *sums, loaded = call(
                functools.partial(second_kernel, key, shape),
                [*outs, like[0]],
                near_k_v_f,
                fars=[q],
                scratch=[pltpu.SemaphoreType.DMA((1,))],
            )
            near_q.append(loaded)
        else:
            phi_k[key], *sums = call(
                functools.partial(later_kernel, len(directions(key)), len(after), key, shape),
                outs,
                [*near_k[:2], *directions(key)],
                after,
            )
        *other, mine = sums
        other = [head_swap(a, 1) for a in other]
        theirs[key], own_sums[key] = other, mine
        piece[key] = call(chip_kernel, whole, [mine, *other])
        got[key] = head_swap(piece[key], key[0] * cores) if key[0] else piece[key]
        return mine

    def directions(key):
        return dirs[key] if key[0] != flip else (near_k[2], near_dirs)

    def inner(key, after=()):
        phi_w[key] = call(
            functools.partial(inner_kernel, len(directions(key)), key, shape),
            [
                per_head(tokens, count),
                jax.ShapeDtypeStruct((cores * group, tokens, 2 * size), F32),
            ],
            [near_q[0], near_k[1], phi_k[key], *directions(key)],
            after,
            scratch=[pltpu.VMEM((cores * group, tokens, tokens), BF16)],
        )
        return phi_w[key][0]

    near_dirs = head_swap(features, 1)
    first = [(flip, dy) for dy in reversed(range(ny))]
    later = [(dx, dy) for dx in range(nx) for dy in reversed(range(ny)) if dx != flip]
    for key in first:
        states(key)
    ready = [piece[first[0]], piece[first[-1]]]
    for ox in range(1, nx):
        if ny == 2:
            part = lax.dynamic_slice_in_dim(features, (position(nx, ny)[2] ^ 1) * group, group, 0)
            (part,) = tie([head_swap(part, ox * cores)], ready)
            rest = seq_swap(part, 1)
            dirs[ox ^ flip, 1] = (part, head_swap(part, 1))
            dirs[ox ^ flip, 0] = (rest,)
        else:
            (full,) = tie([head_swap(features, ox * cores)], ready)
            full = (full, head_swap(full, 1))
            for dy in range(ny):
                dirs[ox ^ flip, dy] = full
    for key in later:
        if key != later[0] and ny == 2:
            (rest,) = tie([dirs[key][0]], [piece[later[0]]])
            dirs[key] = (rest, head_swap(rest, 1))
        states(key, [piece[first[0]]])

    rows_of = {}
    for dy in reversed(range(ny)):
        sums = call(row_kernel, whole, [got[dx, dy] for dx in range(nx)])
        rows_of[dy] = seq_swap(sums, dy) if dy else sums
    summed = call(
        functools.partial(plane_kernel, ny, zrows, ny),
        [jax.ShapeDtypeStruct((zrows + TOTAL_ROWS, count), BF16)] * nz,
        [rows_of[dy] for dy in range(ny)],
        scratch=[pltpu.VMEM((rows, count), F32)],
    )

    def exchange(parts):
        heard = [seq_swap(parts[j], j * ny) for j in reversed(range(1, nz))]
        return [parts[0], *reversed(heard)]

    heard = exchange(summed)
    done = [inner(key, [summed[-1]]) for key in [*first, *later[:-1]]]
    *prefix, totals = call(
        functools.partial(prefix_kernel, nz, zrows, ny),
        [jax.ShapeDtypeStruct((zrows, count), BF16)] * nz
        + [jax.ShapeDtypeStruct((TOTAL_ROWS, count), F32)],
        heard[::-1],
        done,
    )
    done = [inner(later[-1], [prefix[-1]])] if later else []
    prefix = exchange(prefix)
    bases = call(
        functools.partial(rows_kernel, ny, nz, zrows),
        [jax.ShapeDtypeStruct((rows, count), BF16 if dy else F32) for dy in range(ny)],
        [*prefix[::-1], totals, *[rows_of[dy] for dy in range(ny)]],
        done,
        scratch=[pltpu.VMEM((rows, count), F32)],
    )
    result = {}
    for dy, base in enumerate(bases):
        placed = call(
            functools.partial(columns_kernel, nx, ny),
            [whole] * nx,
            [seq_swap(base, dy) if dy else base, *[got[dx, dy] for dx in range(nx)]],
        )
        for dx, a in enumerate(placed):
            result[dx, dy] = head_swap(a, dx * cores) if dx else a

    late = [key for key in plane if all(key)]
    middle = [key for key in plane if key[0] and not key[1]]
    batches = [[(key, 0), (key, 1)] for key in plane if not key[0]]
    batches += [[(key, 0) for key in middle]] if middle else []
    tied = len(batches)
    batches += [[(key, 1) for key in middle] + [(key, 0) for key in late]] if middle else []
    batches += [[(key, 1) for key in late]] if late else []
    out, mark = None, []
    for i, jobs in enumerate(batches):
        args = []
        counts = []
        for key, core in jobs:
            base, extras = result[key], theirs[key]
            if core:
                kernel = functools.partial(far_kernel, shape)
                base = call(kernel, whole, [base, own_sums[key]], mark if key in late else [])
                base, extras = head_swap(base, 1), []
            args += [*phi_w[key], base, *extras]
            counts.append(3 + len(extras))
        marked = [pltpu.VMEM((8, 128), F32)] if i == tied - 1 else []
        out, *marks = call(
            functools.partial(output_kernel, jobs, counts, shape, int(i > 0)),
            [jax.ShapeDtypeStruct((tokens, width), BF16), *marked],
            args,
            [] if out is None else [out],
            [anywhere] + [near] * len(marked),
            [
                pltpu.VMEM((len(jobs), tokens, group * size), BF16),
                pltpu.SemaphoreType.DMA((len(jobs), group)),
            ],
            {} if out is None else {len(args): 0},
        )
        mark = marks or mark
    return out.reshape(queries.shape)


def solution(mesh):
    token = P(None, ("seq", "head"), None)
    return jax.shard_map(
        functools.partial(body, mesh.shape["seq"], mesh.shape["head"]),
        mesh=mesh,
        in_specs=(token, token, token, P("head", None, None)),
        out_specs=token,
        check_vma=False,
    )
```

```python
import functools
import math

import jax
import jax.numpy as jnp
from jax import lax
from jax.experimental import pallas as pl
from jax.experimental.pallas import tpu as pltpu
from jax.sharding import PartitionSpec as P

F32, BF16 = jnp.float32, jnp.bfloat16
LOG2E = math.log2(math.e)
TOTAL_ROWS = 16
VMEM = 6 * 1024 * 1024


def feature_map(x, w):
    size, count = x.shape[1], w.shape[0]
    c = size ** (-0.25)
    p = lax.dot_general(x, w, (((1,), (1,)), ((), ())), preferred_element_type=F32)
    wide = x.astype(F32)
    square = jnp.sum(wide * wide, axis=1, keepdims=True)
    r = lax.rsqrt(square / size + 1e-06)
    half = square * r * r * (0.5 * c * c * LOG2E) + 0.5 * math.log2(count)
    ww = w.astype(F32)
    ww = ww * ww
    high = ww.astype(BF16)
    low = (ww - high.astype(F32)).astype(BF16)
    ones = jnp.ones((16, size), BF16)
    nt = (((1,), (1,)), ((), ()))
    total = lax.dot_general(ones, high, nt, preferred_element_type=F32)
    total = total + lax.dot_general(ones, low, nt, preferred_element_type=F32)
    s = lax.rsqrt(total[:1] / size + 1e-06)
    return jnp.exp2(p * (r * (c * LOG2E)) * s - half).astype(BF16)


def position(nx, ny):
    head, seq = lax.axis_index("head"), lax.axis_index("seq")
    return head // 2, head % 2, seq % ny, seq // ny


def place_of(pos, key, nx, ny, core):
    flip = 1 if nx > 1 else 0
    part = pos[2] ^ key[1]
    return ((pos[0] ^ key[0] ^ flip) * 2 + (pos[1] ^ core)) * ny + part, part


def heads_of(pos, key, shape, f0, *f1):
    nx, ny, group, size = shape
    for core, fs in ((1, f1), (0, [f0])):
        place, part = place_of(pos, key, nx, ny, core)
        held = sum(f.shape[0] for f in fs)
        first = 0 if held == group else part * group
        for h in range(group):
            start = pl.multiple_of((place * group + h) * size, size)
            f, at = fs[0], first + h
            if len(fs) > 1:
                f, at = fs[h // fs[0].shape[0]], h % fs[0].shape[0]
            yield (1 - core) * group + h, pl.ds(start, size), f, at


def states_kernel(key, shape, waits, k, v, fs, phi, *sums):
    nx, ny, group, size = shape
    *others, mine = sums
    pos = position(nx, ny)
    heads = list(heads_of(pos, key, shape, *fs))
    totals = []
    for i, cols, f, at in heads:
        if i % group == 0:
            waits(i // group)
        ph = feature_map(k[:, cols], f[at])
        phi[i] = ph
        totals.append(jnp.sum(ph.astype(F32), axis=0, keepdims=True))
    waits(2)
    for i, cols, _, _ in heads:
        h, out, each = i % group, mine, group // len(others)
        if i < group:
            h, out = h % each, others[h // each]
        st = lax.dot_general(
            v[:, cols], phi[i], (((0,), (0,)), ((), ())), preferred_element_type=F32
        )
        out[h * size : (h + 1) * size] = st.astype(BF16)
    pad = jnp.zeros((TOTAL_ROWS - group, totals[0].shape[1]), F32)
    others[-1][group // len(others) * size :] = jnp.concatenate([*totals[:group], pad], axis=0).astype(BF16)
    mine[group * size :] = jnp.concatenate([*totals[group:], pad], axis=0).astype(BF16)
    waits(3)


def first_kernel(key, shape, k_far, v_far, f_far, f1, *refs):
    nx, ny, group, size = shape
    *outs, k, v, f, sems = refs
    wide = group * size
    blocks = k.shape[1] // wide
    place = place_of(position(nx, ny), key, nx, ny, 0)[0]
    copies = [[], [], [], []]

    def fetch(stage, source, target, at):
        copy = pltpu.make_async_copy(source, target, sems.at[at])
        copy.start()
        copies[stage].append(copy)

    def fetch_block(stage, source, target, j, at):
        cols = pl.ds(pl.multiple_of((place ^ j) * wide, wide), wide)
        fetch(stage, source.at[:, cols], target.at[:, cols], at)

    fetch_block(0, k_far, k, ny, 1)
    fetch(1, f_far, f, 0)
    fetch_block(1, k_far, k, 0, 2)
    fetch_block(2, v_far, v, ny, blocks + 1)
    fetch_block(2, v_far, v, 0, blocks + 2)
    rest = [j for j in range(blocks) if j not in (0, ny)]
    for n, j in enumerate(rest):
        fetch_block(3, k_far, k, j, 3 + n)
        fetch_block(3, v_far, v, j, blocks + 3 + n)

    def waits(stage):
        for copy in copies[stage]:
            copy.wait()

    states_kernel(key, shape, waits, k, v, [f, f1], *outs)


def second_kernel(key, shape, q_far, k, v, f0, f1, *refs):
    *outs, q, sem = refs
    copy = pltpu.make_async_copy(q_far, q, sem.at[0])
    copy.start()

    def waits(stage):
        if stage == 3:
            copy.wait()

    states_kernel(key, shape, waits, k, v, [f0, f1], *outs)


def later_kernel(count, extra, key, shape, k, v, *refs):
    fs, outs = refs[:count], refs[count + extra :]
    states_kernel(key, shape, lambda stage: None, k, v, fs, *outs)


def inner_kernel(count, key, shape, q, v, phi_k, *rest):
    phi_q, inner, weights = rest[-3:]
    nx, ny, group, size = shape
    tokens = q.shape[0]
    heads = list(heads_of(position(nx, ny), key, shape, *rest[:count]))
    for i, cols, f, at in heads:
        phi_q[i] = feature_map(q[:, cols], f[at])
    row = lax.broadcasted_iota(jnp.int32, (tokens, tokens), 0)
    col = lax.broadcasted_iota(jnp.int32, (tokens, tokens), 1)
    mask = col <= row
    for i, _, _, _ in heads:
        sc = lax.dot_general(
            phi_q[i], phi_k[i], (((1,), (1,)), ((), ())), preferred_element_type=F32
        )
        weights[i] = jnp.where(mask, sc, 0.0).astype(BF16)
    ones = jnp.ones((tokens, size), BF16)
    for i, cols, _, _ in heads:
        inner[i] = jnp.dot(
            weights[i],
            jnp.concatenate([v[:, cols], ones], axis=1),
            preferred_element_type=F32,
        )


def output_kernel(jobs, counts, shape, extra, *refs):
    jobs_refs, at = [], 0
    for count in counts:
        jobs_refs.append(refs[at : at + count])
        at += count
    out, *marks, ready, sems = refs[at + extra :]
    nx, ny, group, size = shape
    pos = position(nx, ny)
    add = (pos[1] == 1).astype(F32)
    copies = []
    for n, (key, core) in enumerate(jobs):
        phi_q, inner, base, *extras = jobs_refs[n]
        count = phi_q.shape[-1]
        place = place_of(pos, key, nx, ny, core)[0]
        each = group // max(len(extras), 1)
        totals = base[group * size :].astype(F32)
        if extras:
            totals = totals + add * extras[-1][each * size :].astype(F32)
        for h in range(group):
            rows = slice(h * size, (h + 1) * size)
            st = base[rows]
            if extras:
                extra = extras[h // each][h % each * size : (h % each + 1) * size]
                st = (st.astype(F32) + add * extra.astype(F32)).astype(BF16)
            tot = jnp.broadcast_to(totals[h : h + 1], (size, count)).astype(BF16)
            at = (1 - core) * group + h
            acc = inner[at] + lax.dot_general(
                phi_q[at],
                jnp.concatenate([st, tot], axis=0),
                (((1,), (1,)), ((), ())),
                preferred_element_type=F32,
            )
            ready[n, :, rows] = (acc[:, :size] / acc[:, size:]).astype(BF16)
            start = pl.multiple_of((place * group + h) * size, size)
            copy = pltpu.make_async_copy(
                ready.at[n, :, rows], out.at[:, pl.ds(start, size)], sems.at[n, h]
            )
            copy.start()
            copies.append(copy)
    for mark in marks:
        mark[...] = jnp.zeros(mark.shape, F32)
    for copy in copies:
        copy.wait()


def far_kernel(shape, base, mine, *refs):
    add = (position(*shape[:2])[1] == 0).astype(F32)
    refs[-1][...] = (base[...].astype(F32) + add * mine[...].astype(F32)).astype(BF16)


def tie_kernel(count, *refs):
    for a, out in zip(refs[:count], refs[-count:]):
        out[...] = a[...]


def chip_kernel(mine, *refs):
    *others, out = refs
    start = 0
    for other in others:
        rows = slice(start, start + other.shape[0])
        start = rows.stop
        out[rows] = (mine[rows].astype(F32) + other[...].astype(F32)).astype(BF16)


def row_kernel(*refs):
    *pieces, out = refs
    total = pieces[0][...].astype(F32)
    for piece in pieces[1:]:
        total = total + piece[...].astype(F32)
    out[...] = total.astype(BF16)


def plane_kernel(count, zrows, ny, *refs):
    held, z = refs[-1], position(1, ny)[3]
    pieces, outs = refs[:count], refs[-1 - (held.shape[0] - TOTAL_ROWS) // zrows : -1]
    total = pieces[0][...].astype(F32)
    for piece in pieces[1:]:
        total = total + piece[...].astype(F32)
    held[...] = total
    srows = len(outs) * zrows
    for j, out in enumerate(outs):
        start = pl.multiple_of((z ^ j) * zrows, zrows)
        out[:zrows] = held[pl.ds(start, zrows)].astype(BF16)
        out[zrows:] = held[srows:].astype(BF16)


def prefix_kernel(count, zrows, ny, *refs):
    heard, outs, totals = refs[count - 1 :: -1], refs[-1 - count : -1], refs[-1]
    z = position(1, ny)[3]
    for j, out in enumerate(outs):
        total = jnp.zeros(out.shape, F32)
        for i, part in enumerate(heard):
            total = total + jnp.where((z ^ i) < (z ^ j), part[:zrows].astype(F32), 0.0)
        out[...] = total.astype(BF16)
    total = jnp.zeros(totals.shape, F32)
    for i, part in enumerate(heard):
        total = total + jnp.where((z ^ i) < z, part[zrows:].astype(F32), 0.0)
    totals[...] = total


def rows_kernel(ny, count, zrows, *refs):
    prefix, totals = refs[count - 1 :: -1], refs[count]
    row_sums, outs, held = refs[count + 1 : count + 1 + ny], refs[-1 - ny : -1], refs[-1]
    _, _, y, z = position(1, ny)
    for j in range(count):
        start = pl.multiple_of((z ^ j) * zrows, zrows)
        held[pl.ds(start, zrows)] = prefix[j][...].astype(F32)
    held[count * zrows :] = totals[...]
    for dy, out in enumerate(outs):
        total = held[...]
        for ey, row_sum in enumerate(row_sums):
            if ey != dy:
                total = total + jnp.where((y ^ ey) < (y ^ dy), row_sum[...].astype(F32), 0.0)
        out[...] = total.astype(out.dtype)


def columns_kernel(nx, ny, base, *refs):
    pieces, outs = refs[:nx], refs[nx:]
    x = position(nx, ny)[0]
    for dx, out in enumerate(outs):
        total = base[...].astype(F32)
        for ex, piece in enumerate(pieces):
            if ex != dx:
                total = total + jnp.where((x ^ ex) < (x ^ dx), piece[...].astype(F32), 0.0)
        out[...] = total.astype(BF16)


def body(seqs, heads, queries, keys, values, features):
    tokens, width = queries.shape[1:]
    q, k, v = (a.reshape(tokens, width) for a in (queries, keys, values))
    own, count, size = features.shape
    cores = 2
    nx = heads // cores
    ny = nx if seqs % nx == 0 else 1
    nz = seqs // ny
    flip = 1 if nx > 1 else 0
    group = own // ny
    srows = group * size
    zrows = srows // nz
    rows = srows + TOTAL_ROWS
    plane = [(dx, dy) for dx in range(nx) for dy in range(ny)]


    def head_swap(a, bits):
        return lax.ppermute(a, "head", [(i, i ^ bits) for i in range(heads)])

    def seq_swap(a, bits):
        return lax.ppermute(a, "seq", [(i, i ^ bits) for i in range(seqs)])

    def plane_swap(a, dx, dy):
        if dy == 0:
            return head_swap(a, dx * cores)
        if dx == 0:
            return seq_swap(a, dy)
        pairs = [
            (s * heads + h, (s ^ dy) * heads + (h ^ (dx * cores)))
            for s in range(seqs)
            for h in range(heads)
        ]
        return lax.ppermute(a, ("seq", "head"), pairs)

    anywhere = pl.BlockSpec(memory_space=pl.ANY)

    shape = (nx, ny, group, size)
    near = pl.BlockSpec(memory_space=pltpu.VMEM)
    far = pl.BlockSpec(memory_space=pltpu.HBM)

    def call(kernel, out, args, after=(), outs=near, scratch=(), alias={}, fars=()):
        held = [pltpu.with_memory_space_constraint(a, pltpu.VMEM) for a in args]
        there = [pltpu.with_memory_space_constraint(a, pltpu.HBM) for a in fars]
        if outs is near:
            out = jax.tree.map(lambda a: pltpu.VMEM(a.shape, a.dtype), out)
        return pl.pallas_call(
            kernel,
            out_shape=out,
            in_specs=[far] * len(there) + [near] * len(held) + [anywhere] * len(after),
            out_specs=jax.tree.map(lambda _: outs, out) if outs is near else outs,
            scratch_shapes=scratch,
            input_output_aliases=alias,
            compiler_params=pltpu.CompilerParams(vmem_limit_bytes=VMEM),
        )(*there, *held, *after)

    def tie(arrays, after):
        kernel = functools.partial(tie_kernel, len(arrays))
        return call(kernel, [jax.ShapeDtypeStruct(a.shape, a.dtype) for a in arrays], arrays, after)

    def per_head(a, b):
        return jax.ShapeDtypeStruct((cores * group, a, b), BF16)

    whole = jax.ShapeDtypeStruct((rows, count), BF16)

    dirs, phi_k, phi_w, piece, got, theirs = {}, {}, {}, {}, {}, {}
    near_k, near_q, own_sums = [], [], {}

    def states(key, after=()):
        cuts = group if key == later[0] else min(group, 2)
        cut = [group // cuts * size] * cuts
        cut[-1] += TOTAL_ROWS
        cut = [jax.ShapeDtypeStruct((n, count), BF16) for n in cut]
        outs = [per_head(tokens, count), *cut, whole]
        like = [jax.ShapeDtypeStruct(a.shape, BF16) for a in (k, v, features)]
        if not near_k:
            sems = pltpu.SemaphoreType.DMA((2 * (width // (group * size)) + 1,))
            phi_k[key], *sums, key_block, value_block, part = call(
                functools.partial(first_kernel, key, shape),
                outs + like,
                [near_dirs],
                fars=[k, v, features],
                scratch=[sems],
            )
            near_k.extend([key_block, value_block, part])
        elif not near_q:
            near_k_v_f = [near_k[0], near_k[1], near_k[2], near_dirs]
            phi_k[key], *sums, loaded = call(
                functools.partial(second_kernel, key, shape),
                [*outs, like[0]],
                near_k_v_f,
                fars=[q],
                scratch=[pltpu.SemaphoreType.DMA((1,))],
            )
            near_q.append(loaded)
        else:
            phi_k[key], *sums = call(
                functools.partial(later_kernel, len(directions(key)), len(after), key, shape),
                outs,
                [*near_k[:2], *directions(key)],
                after,
            )
        *other, mine = sums
        other = [head_swap(a, 1) for a in other]
        theirs[key], own_sums[key] = other, mine
        piece[key] = call(chip_kernel, whole, [mine, *other])
        got[key] = head_swap(piece[key], key[0] * cores) if key[0] else piece[key]
        return mine

    def directions(key):
        return dirs[key] if key[0] != flip else (near_k[2], near_dirs)

    def inner(key, after=()):
        phi_w[key] = call(
            functools.partial(inner_kernel, len(directions(key)), key, shape),
            [
                per_head(tokens, count),
                jax.ShapeDtypeStruct((cores * group, tokens, 2 * size), F32),
            ],
            [near_q[0], near_k[1], phi_k[key], *directions(key)],
            after,
            scratch=[pltpu.VMEM((cores * group, tokens, tokens), BF16)],
        )
        return phi_w[key][0]

    near_dirs = head_swap(features, 1)
    first = [(flip, dy) for dy in reversed(range(ny))]
    later = [(dx, dy) for dx in range(nx) for dy in reversed(range(ny)) if dx != flip]
    for key in first:
        states(key)
    ready = [piece[first[0]], piece[first[-1]]]
    for ox in range(1, nx):
        if ny == 2:
            part = lax.dynamic_slice_in_dim(features, (position(nx, ny)[2] ^ 1) * group, group, 0)
            (part,) = tie([head_swap(part, ox * cores)], ready)
            rest = seq_swap(part, 1)
            dirs[ox ^ flip, 1] = (part, head_swap(part, 1))
            dirs[ox ^ flip, 0] = (rest,)
        else:
            (full,) = tie([head_swap(features, ox * cores)], ready)
            full = (full, head_swap(full, 1))
            for dy in range(ny):
                dirs[ox ^ flip, dy] = full
    for key in later:
        if key != later[0] and ny == 2:
            (rest,) = tie([dirs[key][0]], [piece[later[0]]])
            dirs[key] = (rest, head_swap(rest, 1))
        states(key, [])

    rows_of = {}
    for dy in reversed(range(ny)):
        sums = call(row_kernel, whole, [got[dx, dy] for dx in range(nx)])
        rows_of[dy] = seq_swap(sums, dy) if dy else sums
    summed = call(
        functools.partial(plane_kernel, ny, zrows, ny),
        [jax.ShapeDtypeStruct((zrows + TOTAL_ROWS, count), BF16)] * nz,
        [rows_of[dy] for dy in range(ny)],
        scratch=[pltpu.VMEM((rows, count), F32)],
    )

    def exchange(parts):
        heard = [seq_swap(parts[j], j * ny) for j in reversed(range(1, nz))]
        return [parts[0], *reversed(heard)]

    heard = exchange(summed)
    done = [inner(key, [summed[-1]]) for key in [*first, *later[:-1]]]
    *prefix, totals = call(
        functools.partial(prefix_kernel, nz, zrows, ny),
        [jax.ShapeDtypeStruct((zrows, count), BF16)] * nz
        + [jax.ShapeDtypeStruct((TOTAL_ROWS, count), F32)],
        heard[::-1],
        done,
    )
    done = [inner(later[-1], [prefix[-1]])] if later else []
    prefix = exchange(prefix)
    bases = call(
        functools.partial(rows_kernel, ny, nz, zrows),
        [jax.ShapeDtypeStruct((rows, count), BF16 if dy else F32) for dy in range(ny)],
        [*prefix[::-1], totals, *[rows_of[dy] for dy in range(ny)]],
        done,
        scratch=[pltpu.VMEM((rows, count), F32)],
    )
    result = {}
    for dy, base in enumerate(bases):
        placed = call(
            functools.partial(columns_kernel, nx, ny),
            [whole] * nx,
            [seq_swap(base, dy) if dy else base, *[got[dx, dy] for dx in range(nx)]],
        )
        for dx, a in enumerate(placed):
            result[dx, dy] = head_swap(a, dx * cores) if dx else a

    late = [key for key in plane if all(key)]
    middle = [key for key in plane if key[0] and not key[1]]
    batches = [[(key, 0), (key, 1)] for key in plane if not key[0]]
    batches += [[(key, 0) for key in middle]] if middle else []
    tied = len(batches)
    batches += [[(key, 1) for key in middle] + [(key, 0) for key in late]] if middle else []
    batches += [[(key, 1) for key in late]] if late else []
    out, mark = None, []
    for i, jobs in enumerate(batches):
        args = []
        counts = []
        for key, core in jobs:
            base, extras = result[key], theirs[key]
            if core:
                kernel = functools.partial(far_kernel, shape)
                base = call(kernel, whole, [base, own_sums[key]], mark if key in late else [])
                base, extras = head_swap(base, 1), []
            args += [*phi_w[key], base, *extras]
            counts.append(3 + len(extras))
        marked = [pltpu.VMEM((8, 128), F32)] if i == tied - 1 else []
        out, *marks = call(
            functools.partial(output_kernel, jobs, counts, shape, int(i > 0)),
            [jax.ShapeDtypeStruct((tokens, width), BF16), *marked],
            args,
            [] if out is None else [out],
            [anywhere] + [near] * len(marked),
            [
                pltpu.VMEM((len(jobs), tokens, group * size), BF16),
                pltpu.SemaphoreType.DMA((len(jobs), group)),
            ],
            {} if out is None else {len(args): 0},
        )
        mark = marks or mark
    return out.reshape(queries.shape)


def solution(mesh):
    token = P(None, ("seq", "head"), None)
    return jax.shard_map(
        functools.partial(body, mesh.shape["seq"], mesh.shape["head"]),
        mesh=mesh,
        in_specs=(token, token, token, P("head", None, None)),
        out_specs=token,
        check_vma=False,
    )
```
